32 devices in a mesh: groups: 2 (over y), dp: 4 (over z), owner: 2 (over x), sub: 2 (over core).
Axes of the slice: x: 2, y: 2, z: 4, core: 2. Of those that a mesh axis runs over, the one named last changes fastest.
Arguments:
- ex_acts: bfloat16 [48, 16, 5120], P(('groups', 'dp'), None, ('owner', 'sub')), parts along dimension 0, may hold values from -6 to 6
- ex_grads: bfloat16 [48, 16, 8, 1280], P(('groups', 'dp'), None, 'owner', 'sub'), parts along dimension 0, may hold values from -0.008972168 to 0.008972168
- ex_mask: int32 [48, 16], P(('groups', 'dp')), parts along dimension 0, may hold values 0 or 1
- ex_ids: int32 [48], P(('groups', 'dp')), parts along dimension 0, may hold values from 0 to 23, each once
- query_acts: bfloat16 [32, 16, 5120], P('groups', None, ('owner', 'sub')), parts along dimension 0, may hold values from -6 to 6
- query_grads: bfloat16 [32, 16, 8, 1280], P('groups', None, 'owner', 'sub'), parts along dimension 0, may hold values from -0.008972168 to 0.008972168
- input_basis: bfloat16 [5120, 5120], P(('owner', 'sub'), 'dp'), may hold values from -0.078125 to 0.078125
- hidden_basis: bfloat16 [8, 1280, 1280], P('owner', 'dp', 'sub'), may hold values from -0.15625 to 0.15625
- eigenvalues: float32 [5120, 8, 1280], P('dp', 'owner', 'sub'), may hold values from 0.05 to 5
Outputs:
- scores: float32 [32, 24], P('groups', 'dp'), parts along dimension 0
The draws below stay inside these ranges and needn't reach their ends.
There are 2 independent parts, one for each index of `groups`. The reference program is written for one: setup_inputs(seed, part) draws one part's arguments, and reference() takes and returns one part's arrays. A program takes and returns all parts, laid end to end along the dimension named above; an argument that names none is the same for every part. Nothing has to cross between parts.
Inputs may be any that keep to these rules, and one draw needn't show every extreme that they name: `ex_mask`: 1 keeps a token position, 0 drops it. A permutation: the example at position n is scored in column ex_ids[n].
All inputs are finite; a program needn't handle non-finite values. No bound on the sum of `ex_mask` on one device may be relied on, other than what follows from the above.
Results may differ from the reference program's by a relative error of at most 0.0052.
Values may be sent and summed in bfloat16 or wider, within the bound.
No kernel may reach another device: no remote copies, remote signals or barrier semaphores. Data moves between devices by JAX's collectives and lax.ppermute only.
A program may use at most 448 MiB of HBM per device.

```python
import math
import jax
import jax.numpy as jnp
from jax import lax

D = 5120
HB = 1280
NB = 8
L = 16
Q = 16
LQ = 16
EX = 24


def set_ends(values, key, smallest, largest):
    extent = values.shape
    index_at = [jax.random.randint(jax.random.fold_in(key, axis), (), 0, extent[axis]) for axis in range(len(extent))]
    values = values.at[tuple(index_at)].set(smallest)
    longest = extent.index(max(extent))
    index_at[longest] = (index_at[longest] + 1) % extent[longest]
    return values.at[tuple(index_at)].set(largest)


def level_of(key, dims, split, low, largest):
    loudness, own = 1.0, jax.random.fold_in(key, 6)
    for dim, shards_of in split:
        steps = jnp.exp(jax.random.uniform(jax.random.fold_in(own, dim), (shards_of,), jnp.float32, low / len(split), largest / len(split)))
        loudness = loudness * jnp.repeat(steps, dims[dim] // shards_of).reshape([-1 if axis == dim else 1 for axis in range(len(dims))])
    return loudness


def bell_draw(rng, extent, deviation, limit, shards=(), kind=jnp.bfloat16):
    factor_of = level_of(rng, extent, shards, -0.22, 0.18) if shards else 1.0
    result = jax.random.normal(rng, extent, jnp.float32) * deviation * factor_of
    return jnp.minimum(jnp.maximum(result, -limit), limit).astype(kind)


def setup_inputs(seed: int = 0, part: int = 0) -> dict:
    key_list = jax.random.split(jax.random.key(seed), 10)
    own_keys = jax.random.split(jax.random.fold_in(key_list[9], part), 10)
    return {
        "ex_acts": bell_draw(own_keys[0], (EX, L, D), 1.0, 6.0, ((0, 4), (2, 4))),
        "ex_grads": bell_draw(own_keys[1], (EX, L, NB, HB), 0.0015, 0.008972168, ((0, 4), (2, 2), (3, 2))),
        "ex_mask": set_ends((jax.random.randint(own_keys[2], (EX, L), 0, 4) < 3).astype(jnp.int32), jax.random.fold_in(own_keys[2], 1), 0, 1),
        "ex_ids": jax.random.permutation(own_keys[3], EX).astype(jnp.int32),
        "query_acts": bell_draw(own_keys[4], (Q, LQ, D), 1.0, 6.0, ((2, 4),)),
        "query_grads": bell_draw(own_keys[5], (Q, LQ, NB, HB), 0.0015, 0.008972168, ((2, 2), (3, 2))),
        "input_basis": bell_draw(key_list[6], (D, D), D ** -0.5, 0.078125, ((0, 4), (1, 4))),
        "hidden_basis": bell_draw(key_list[7], (NB, HB, HB), HB ** -0.5, 0.15625, ((0, 2), (1, 4), (2, 2))),
        "eigenvalues": jnp.clip(jnp.exp(math.log(5.0) - 4.6051702 * jax.random.uniform(key_list[8], (D, NB, HB), jnp.float32) ** level_of(key_list[8], (D, NB, HB), ((0, 4), (1, 2), (2, 2)), -0.2, 0.2)), 0.05, 5.0),
    }


DAMP = 0.05


def rotate_in(acts, input_basis):
    flat_rows = acts.reshape(-1, acts.shape[-1])
    return jnp.dot(flat_rows, input_basis, preferred_element_type=jnp.float32).astype(jnp.bfloat16)


def rotate_hidden(grads, hidden_basis):
    flat_rows = grads.reshape(-1, grads.shape[-2], grads.shape[-1]).astype(jnp.float32)
    rotated = jnp.einsum("tbr,brc->tbc", flat_rows, hidden_basis.astype(jnp.float32))
    return rotated.astype(jnp.bfloat16).reshape(flat_rows.shape[0], -1)


def reference(ex_acts, ex_grads, ex_mask, ex_ids, query_acts, query_grads, input_basis, hidden_basis, eigenvalues):
    hidden_width = NB * HB
    keep_mask = ex_mask.astype(ex_grads.dtype)[:, :, None, None]
    masked = ex_grads * keep_mask
    ex_in = rotate_in(ex_acts, input_basis).reshape(EX, L, D)
    ex_hidden = rotate_hidden(masked, hidden_basis).reshape(EX, L, hidden_width)
    query_in = rotate_in(query_acts, input_basis).reshape(Q, LQ, D)
    query_hidden = rotate_hidden(query_grads, hidden_basis).reshape(Q, LQ, hidden_width)
    divisor_all = eigenvalues.reshape(D, hidden_width) + DAMP
    col_block = math.gcd(D, 512)
    num_blocks = D // col_block
    per_group = 8
    ex_groups = EX // per_group
    hidden_groups = ex_hidden.reshape(ex_groups, per_group, L, hidden_width)

    def one_block(summed, block_index):
        first_col = (block_index * col_block).astype(jnp.int32)
        query_blk = lax.dynamic_slice_in_dim(query_in, first_col, col_block, 2)
        divisor = lax.dynamic_slice_in_dim(divisor_all, first_col, col_block, 0)

        def precondition(items):
            acts_one, grads_one = items
            grad_blk = lax.dot_general(acts_one, grads_one, (((0,), (0,)), ((), ())), preferred_element_type=jnp.float32)
            return (grad_blk / divisor).astype(jnp.bfloat16)

        query_pre = lax.map(precondition, (query_blk, query_hidden)).reshape(Q, col_block * hidden_width)
        ex_blk = lax.dynamic_slice_in_dim(ex_in, first_col, col_block, 2).reshape(ex_groups, per_group, L, col_block)

        def score_group(items):
            acts_blk, grads_blk = items
            grad_blk = jnp.einsum("ntj,nti->nji", acts_blk.astype(jnp.float32), grads_blk.astype(jnp.float32))
            grad_blk = grad_blk.astype(jnp.bfloat16).reshape(per_group, col_block * hidden_width)
            return lax.dot_general(query_pre, grad_blk, (((1,), (1,)), ((), ())), preferred_element_type=jnp.float32)

        part_scores = lax.map(score_group, (ex_blk, hidden_groups))
        part_scores = jnp.transpose(part_scores, (1, 0, 2)).reshape(Q, EX)
        return summed + part_scores, None

    summed, _ = lax.scan(one_block, jnp.zeros((Q, EX), jnp.float32), jnp.arange(num_blocks, dtype=jnp.int32))
    onehot = (ex_ids[:, None] == jnp.arange(EX, dtype=jnp.int32)[None, :]).astype(jnp.float32)
    return jnp.dot(summed, onehot, precision=lax.Precision.HIGHEST, preferred_element_type=jnp.float32)
```

```python
import functools

import jax
import jax.numpy as jnp
from jax import lax
from jax.experimental import pallas as pl
from jax.experimental.pallas import tpu as pltpu
from jax.sharding import PartitionSpec as P

DAMP = 0.05
BF = jnp.bfloat16
F32 = jnp.float32


def ring(x, axis, size, shift=1):
    return lax.ppermute(x, axis, [(i, (i + shift) % size) for i in range(size)])


def dot(a, b):
    return jnp.dot(a, b, preferred_element_type=F32)


def col_tiles(width):
    tiles, at = [], 0
    while at < width:
        step = min(256, width - at)
        tiles.append((at, step))
        at += step
    return tiles


def score_kernel(
    n, q_count, seq, share, block,
    idx, ei, qit, w_hbm, basis, q_own, q_oth, e_own, e_oth, *rest,
):
    xs, rest = rest[: n - 1], rest[n - 1 :]
    zs, rest = rest[: n - 1], rest[n - 1 :]
    ys = ()
    if share:
        ys, rest = rest[: n - 1], rest[n - 1 :]
    out, full, tok_own, tok_oth, hid, wv, p0, p1, sems = rest
    dpi, grp, sub = idx[0], idx[1], idx[2]
    rows, width = basis.shape
    half_rows = full.shape[0] // 2
    q_rows, e_rows = q_own.shape[0], e_own.shape[0]
    ex_rows = e_rows * n
    ex_count = ex_rows // seq
    j_rows = ei.shape[1]
    per = 128 // seq
    tiles = col_tiles(width)

    copies = []
    for i, (at, step) in enumerate(tiles):
        copy = pltpu.make_async_copy(
            w_hbm.at[:, pl.ds(block * width + at, step)], wv.at[:, pl.ds(at, step)], sems.at[i]
        )
        copy.start()
        copies.append(copy)

    full[pl.ds(pl.multiple_of(dpi * rows, 16), rows), :] = basis[...]
    piece = rows // 2 if share else rows
    for k in range(1, n):
        src = lax.rem(dpi + n - k, n)
        if share:
            at = src * rows + grp * piece
            full[pl.ds(pl.multiple_of(at, 16), piece), :] = xs[k - 1][e_rows:, :]
            at = src * rows + (1 - grp) * piece
            full[pl.ds(pl.multiple_of(at, 16), piece), :] = ys[k - 1][e_rows:, :]
        else:
            full[pl.ds(pl.multiple_of(src * rows, 16), piece), :] = xs[k - 1][e_rows:, :]
    tok_own[:q_rows, :] = q_own[...]
    tok_oth[:q_rows, :] = q_oth[...]
    tok_own[q_rows : q_rows + e_rows, :] = e_own[...]
    tok_oth[q_rows : q_rows + e_rows, :] = e_oth[...]
    for k in range(1, n):
        at = q_rows + k * e_rows
        tok_own[at : at + e_rows, :] = xs[k - 1][:e_rows, :]
        tok_oth[at : at + e_rows, :] = zs[k - 1][:e_rows, :]
    b_own = full[pl.ds(pl.multiple_of(sub * half_rows, 16), half_rows), :]
    b_oth = full[pl.ds(pl.multiple_of((1 - sub) * half_rows, 16), half_rows), :]
    hid[...] = (dot(tok_own[...], b_own) + dot(tok_oth[...], b_oth)).astype(BF)

    m_step = j_rows // 2 if j_rows % 32 == 0 else j_rows
    out[...] = jnp.zeros_like(out)
    for i, (at, step) in enumerate(tiles):
        copies[i].wait()

        def outer(q, dst):
            grp_q = q // per
            rhs = hid[pl.ds(pl.multiple_of(grp_q * 128, 128), 128), at : at + step]
            row = lax.broadcasted_iota(jnp.int32, (128, step), 0) // seq
            rhs = jnp.where(row == q - grp_q * per, rhs.astype(F32), 0.0).astype(BF)
            for m in range(0, j_rows, m_step):
                grad = dot(qit[grp_q, m : m + m_step, :], rhs)
                dst[m : m + m_step, :step] = (grad * wv[m : m + m_step, at : at + step]).astype(BF)

        def score(q, src):
            prod = dot(ei[...], src[:, :step]) * hid[q_rows:, at : at + step].astype(F32)
            if step > 128:
                prod = prod[:, :128] + prod[:, 128:]
            out[q] += prod.reshape(ex_count, seq // 8, 8, 128).sum(1)

        outer(0, p0)

        def pair(i, carry):
            q = 2 * i
            outer(q + 1, p1)
            score(q, p0)
            outer(q + 2, p0)
            score(q + 1, p1)
            return carry

        lax.fori_loop(0, q_count // 2 - 1, pair, 0)
        outer(q_count - 1, p1)
        score(q_count - 2, p0)
        score(q_count - 1, p1)


def block_scores(n, q_count, seq, share, block, idx, ei, qit, w, basis, q_own, q_oth, e_own, e_oth, xs, zs, ys):
    rows, width = basis.shape
    j_rows = ei.shape[1]
    ex_rows = ei.shape[0]
    q_rows = q_own.shape[0]
    ex_count = ex_rows // seq
    vmem = pl.BlockSpec(memory_space=pltpu.VMEM)
    ops = (ei, qit, w, basis, q_own, q_oth, e_own, e_oth, *xs, *zs, *ys)
    specs = [vmem, vmem, pl.BlockSpec(memory_space=pl.ANY)] + [vmem] * (len(ops) - 3)
    flops = 2 * q_count * j_rows * width * (256 + ex_rows)
    return pl.pallas_call(
        functools.partial(score_kernel, n, q_count, seq, share, block),
        out_shape=jax.ShapeDtypeStruct((q_count, ex_count, 8, 128), F32),
        in_specs=[pl.BlockSpec(memory_space=pltpu.SMEM)] + specs,
        out_specs=vmem,
        scratch_shapes=[
            pltpu.VMEM((rows * n, width), BF),
            pltpu.VMEM((q_rows + ex_rows, width), BF),
            pltpu.VMEM((q_rows + ex_rows, width), BF),
            pltpu.VMEM((q_rows + ex_rows, width), BF),
            pltpu.VMEM((j_rows, width), F32),
            pltpu.VMEM((j_rows, 256), BF),
            pltpu.VMEM((j_rows, 256), BF),
            pltpu.SemaphoreType.DMA((len(col_tiles(width)),)),
        ],
        compiler_params=pltpu.CompilerParams(vmem_limit_bytes=48 * 1024 * 1024),
        cost_estimate=pl.CostEstimate(flops=flops, bytes_accessed=8 * 2**20, transcendentals=0),
        name="block_scores",
    )(idx, *ops)


def swap(x, axis):
    return lax.ppermute(x, axis, [(0, 1), (1, 0)])


def sum_features(part, sub, sizes):
    half = part.shape[0] // 2
    mine = lax.dynamic_slice_in_dim(part, sub * half, half, 0)
    other = lax.dynamic_slice_in_dim(part, (1 - sub) * half, half, 0).astype(BF)
    mine = mine + swap(other, "sub").astype(F32)
    if sizes["owner"] == 2:
        total = mine + swap(mine.astype(BF), "owner").astype(F32)
    else:
        total = lax.psum(mine, "owner")
    total = total.astype(BF)
    rest = swap(total, "sub")
    return jnp.where(
        sub == 0, jnp.concatenate([total, rest], 0), jnp.concatenate([rest, total], 0)
    )


def shards(
    sizes,
    ex_acts,
    ex_grads,
    ex_mask,
    ex_ids,
    query_acts,
    query_grads,
    input_basis,
    hidden_basis,
    eigenvalues,
):
    n = sizes["dp"]
    dpi, grp, sub = (lax.axis_index(a) for a in ("dp", "groups", "sub"))
    ex_count, seq, input_cols = ex_acts.shape
    q_count, q_seq, _ = query_acts.shape
    blocks, rows, width = hidden_basis.shape
    j_rows = input_basis.shape[1]
    e_rows, q_rows = ex_count * seq, q_count * q_seq
    share = sizes["groups"] == 2 and rows % 32 == 0
    idx = jnp.stack([dpi, grp, sub]).astype(jnp.int32)

    keep = ex_mask.astype(BF).reshape(e_rows, 1)
    acts = [ex_acts.reshape(e_rows, input_cols) * keep]
    ids = [ex_ids]
    for _ in range(n - 1):
        acts.append(ring(acts[-1], "dp", n))
        ids.append(ring(ids[-1], "dp", n))
    all_ids = jnp.concatenate(ids)

    e_raw = jnp.transpose(ex_grads.reshape(e_rows, blocks, width), (1, 0, 2))
    q_raw = jnp.transpose(query_grads.reshape(q_rows, blocks, width), (1, 0, 2))
    e_oth, q_oth = swap(e_raw, "sub"), swap(q_raw, "sub")
    piece = rows // 2 if share else rows
    mine = lax.dynamic_slice_in_dim(hidden_basis, grp * piece, piece, 1) if share else hidden_basis
    xs, ys, zs = [], [], []
    for b in range(blocks):
        last = jnp.concatenate([e_raw[b], mine[b]], 0)
        xb, yb, zb = [], [], []
        for _ in range(n - 1):
            last = ring(last, "dp", n)
            xb.append(last)
            zb.append(swap(last, "sub"))
            if share:
                yb.append(swap(last, "groups"))
        xs.append(xb)
        ys.append(yb)
        zs.append(zb)

    q_in = sum_features(dot(query_acts.reshape(q_rows, input_cols), input_basis), sub, sizes)
    ei = sum_features(dot(jnp.concatenate(acts, 0), input_basis), sub, sizes)
    qit = jnp.transpose(q_in.reshape(q_rows // 128, 128, j_rows), (0, 2, 1))
    w = (1.0 / (eigenvalues + DAMP)).reshape(j_rows, blocks * width)

    total = 0.0
    for b in range(blocks):
        total = total + block_scores(
            n, q_count, seq, share, b, idx, ei, qit, w, hidden_basis[b],
            q_raw[b], q_oth[b], e_raw[b], e_oth[b], xs[b], zs[b], ys[b],
        )
    scores = total.sum((2, 3))

    ex_total = all_ids.shape[0]
    onehot = (all_ids[:, None] == jnp.arange(ex_total, dtype=jnp.int32)[None, :]).astype(F32)
    placed = jnp.dot(scores, onehot, precision=lax.Precision.HIGHEST, preferred_element_type=F32)
    placed = placed + swap(placed, "sub")
    if sizes["owner"] == 2:
        placed = placed + swap(placed, "owner")
    else:
        placed = lax.psum(placed, "owner")

    def columns(device):
        return lax.dynamic_slice_in_dim(placed, lax.rem(device, n) * ex_count, ex_count, 1)

    result = columns(dpi)
    for k in range(1, n):
        result = result + ring(columns(dpi + k), "dp", n, k)
    return result


def solution(mesh):
    in_specs = (
        P(("groups", "dp"), None, ("owner", "sub")),
        P(("groups", "dp"), None, "owner", "sub"),
        P(("groups", "dp"), None),
        P(("groups", "dp")),
        P("groups", None, ("owner", "sub")),
        P("groups", None, "owner", "sub"),
        P(("owner", "sub"), "dp"),
        P("owner", "dp", "sub"),
        P("dp", "owner", "sub"),
    )
    out_specs = P("groups", "dp")
    body = functools.partial(shards, dict(mesh.shape))
    return jax.shard_map(body, mesh=mesh, in_specs=in_specs, out_specs=out_specs, check_vma=False)
```

```python
import functools

import jax
import jax.numpy as jnp
from jax import lax
from jax.experimental import pallas as pl
from jax.experimental.pallas import tpu as pltpu
from jax.sharding import PartitionSpec as P

DAMP = 0.05
BF = jnp.bfloat16
F32 = jnp.float32
MIB = 1024 * 1024
ANY = pl.BlockSpec(memory_space=pl.ANY)
VMEM = pl.BlockSpec(memory_space=pltpu.VMEM)
SMEM = pl.BlockSpec(memory_space=pltpu.SMEM)


def dot(a, b):
    return jnp.dot(a, b, preferred_element_type=F32)


def swap(x, axis):
    return lax.ppermute(x, axis, [(0, 1), (1, 0)])


def gather_parts(n):
    if n == 4:
        return [
            (1, lambda me: me ^ 1, None),
            (2, lambda me: me ^ 2, None),
            (3, lambda me: me ^ 3, (1, 2)),
            (3, lambda me: me ^ 3, (0, 3)),
        ]
    return [(k, lambda me, k=k: lax.rem(me + n - k, n), None) for k in range(1, n)]


def gather(x, n):
    if n == 4:
        near = lax.ppermute(x, "dp", [(i, i ^ 1) for i in range(4)])
        far = lax.ppermute(x, "dp", [(i, i ^ 2) for i in range(4)])
        middle = lax.ppermute(x, "dp", [(1, 2), (2, 1)])
        ends = lax.ppermute(far, "dp", [(1, 0), (2, 3)])
        return [near, far, middle, ends]
    parts = [x]
    for _ in range(n - 1):
        parts.append(lax.ppermute(parts[-1], "dp", [(i, (i + 1) % n) for i in range(n)]))
    return parts[1:]


def swap_part(x, axis, n, where):
    if where is None:
        return swap(x, axis)
    if axis == "groups":
        pairs = [(g * n + z, (1 - g) * n + z) for g in (0, 1) for z in where]
        return lax.ppermute(x, ("groups", "dp"), pairs)
    pairs = [(z * 2 + s, z * 2 + 1 - s) for s in (0, 1) for z in where]
    return lax.ppermute(x, ("dp", "sub"), pairs)


def whole(x, parts, n, dpi):
    rows = [x]
    for part, (pos, _, where) in zip(parts, gather_parts(n)):
        if pos < len(rows):
            here = (dpi == where[0]) | (dpi == where[1])
            rows[pos] = jnp.where(here, part, rows[pos])
        else:
            rows.append(part)
    return jnp.concatenate(rows, 0)


def at_part(where, dpi, run):
    if where is None:
        run()
    else:
        pl.when((dpi == where[0]) | (dpi == where[1]))(run)


def prep_kernel(blocks, piece, share, idx, e_grads, q_grads, basis, *rest):
    pays, q_raw, sem = rest[:blocks], rest[blocks], rest[blocks + 1]
    e_rows = e_grads.shape[0]
    first = idx[1] * piece if share else 0
    copies = []
    for b in range(blocks):
        copy = pltpu.make_async_copy(
            basis.at[b, pl.ds(pl.multiple_of(first, 16), piece), :],
            pays[b].at[pl.ds(e_rows, piece), :],
            sem.at[b],
        )
        copy.start()
        copies.append(copy)
    for b in range(blocks):
        pays[b][:e_rows, :] = e_grads[:, b, :]
        q_raw[b] = q_grads[:, b, :]
    for copy in copies:
        copy.wait()


def prepare(idx, e_grads, q_grads, basis, piece, share):
    e_rows, blocks, width = e_grads.shape
    q_rows = q_grads.shape[0]
    pay = jax.ShapeDtypeStruct((e_rows + piece, width), BF)
    out = pl.pallas_call(
        functools.partial(prep_kernel, blocks, piece, share),
        out_shape=[pay] * blocks + [jax.ShapeDtypeStruct((blocks, q_rows, width), BF)],
        in_specs=[SMEM, VMEM, VMEM, ANY],
        out_specs=[VMEM] * (blocks + 1),
        scratch_shapes=[pltpu.SemaphoreType.DMA((blocks,))],
        compiler_params=pltpu.CompilerParams(vmem_limit_bytes=24 * MIB),
        cost_estimate=pl.CostEstimate(flops=0, bytes_accessed=6 * MIB, transcendentals=0),
        name="prepare",
    )(idx, e_grads, q_grads, basis)
    return out[:blocks], out[blocks]


def weight_kernel(blocks, step, lam, w, buf, sems):
    i, count = pl.program_id(0), pl.num_programs(0)
    per = count // blocks

    def copy(j, slot):
        def go(b):
            return pltpu.make_async_copy(
                lam.at[pl.ds(pl.multiple_of(lax.rem(j, per) * step, 8), step), b, :],
                buf.at[slot],
                sems.at[slot],
            )
        return go

    def start(j, slot):
        for b in range(blocks):
            pl.when(j // per == b)(lambda b=b: copy(j, slot)(b).start())

    @pl.when(i == 0)
    def _():
        start(i, 0)

    @pl.when(i + 1 < count)
    def _():
        start(i + 1, lax.rem(i + 1, 2))

    slot = lax.rem(i, 2)
    copy(i, slot)(0).wait()
    w[...] = 1.0 / (buf[slot] + DAMP)


def weights(lam):
    j_rows, blocks, width = lam.shape
    step = 320 if j_rows % 320 == 0 else j_rows
    return pl.pallas_call(
        functools.partial(weight_kernel, blocks, step),
        grid=(blocks * (j_rows // step),),
        out_shape=jax.ShapeDtypeStruct((blocks * j_rows, width), F32),
        in_specs=[ANY],
        out_specs=pl.BlockSpec((step, width), lambda i: (i, 0)),
        scratch_shapes=[pltpu.VMEM((2, step, width), F32), pltpu.SemaphoreType.DMA((2,))],
        compiler_params=pltpu.CompilerParams(vmem_limit_bytes=24 * MIB),
        cost_estimate=pl.CostEstimate(
            flops=4 * lam.size, bytes_accessed=8 * lam.size, transcendentals=0
        ),
        name="weights",
    )(lam)


def score_kernel(n, q_count, seq, share, block, e_rows, idx, ei, qit, w, basis, q_own, q_oth, *rest):
    parts = gather_parts(n)
    count = len(parts)
    xs, rest = rest[: count + 1], rest[count + 1 :]
    zs, rest = rest[: count + 1], rest[count + 1 :]
    ys = ()
    if share:
        ys, rest = rest[:count], rest[count:]
    out, full, tok_own, tok_oth, hid, wv, p0, p1, acc, sems, w_sem = rest
    dpi, grp, sub = idx[0], idx[1], idx[2]
    rows, width = basis.shape[1], basis.shape[2]
    half_rows = full.shape[0] // 2
    q_rows = q_own.shape[1]
    j_rows = ei.shape[1]
    ex_count = ei.shape[0] // seq
    per = 128 // seq
    piece = rows // 2 if share else rows

    w_copy = pltpu.make_async_copy(w.at[pl.ds(block * j_rows, j_rows), :], wv, w_sem)

    def basis_rows(at, length):
        return full.at[pl.ds(pl.multiple_of(at, 16), length), :]

    moves = [
        (None, q_own.at[block], tok_own.at[pl.ds(0, q_rows), :]),
        (None, q_oth.at[block], tok_oth.at[pl.ds(0, q_rows), :]),
        (None, basis.at[block], basis_rows(dpi * rows, rows)),
        (None, xs[0].at[pl.ds(0, e_rows), :], tok_own.at[pl.ds(q_rows, e_rows), :]),
        (None, zs[0].at[pl.ds(0, e_rows), :], tok_oth.at[pl.ds(q_rows, e_rows), :]),
    ]
    for i, (pos, source, where) in enumerate(parts):
        src = source(dpi)
        to = pl.ds(q_rows + pos * e_rows, e_rows)
        moves.append((where, xs[i + 1].at[pl.ds(0, e_rows), :], tok_own.at[to, :]))
        moves.append((where, zs[i + 1].at[pl.ds(0, e_rows), :], tok_oth.at[to, :]))
        mine = src * rows + grp * piece if share else src * rows
        moves.append((where, xs[i + 1].at[pl.ds(e_rows, piece), :], basis_rows(mine, piece)))
        if share:
            other = src * rows + (1 - grp) * piece
            moves.append((where, ys[i].at[pl.ds(e_rows, piece), :], basis_rows(other, piece)))

    def move(i):
        return pltpu.make_async_copy(moves[i][1], moves[i][2], sems.at[i])

    for i, (where, _, _) in enumerate(moves):
        at_part(where, dpi, lambda i=i: move(i).start())
    w_copy.start()
    acc[...] = jnp.zeros_like(acc)
    for i, (where, _, _) in enumerate(moves):
        at_part(where, dpi, lambda i=i: move(i).wait())

    b_own = full[pl.ds(pl.multiple_of(sub * half_rows, 16), half_rows), :]
    b_oth = full[pl.ds(pl.multiple_of((1 - sub) * half_rows, 16), half_rows), :]
    hid[...] = (dot(tok_own[...], b_own) + dot(tok_oth[...], b_oth)).astype(BF)
    w_copy.wait()

    m_step = j_rows // 2

    def outer_rhs(q):
        grp_q = q // per
        rhs = hid[pl.ds(pl.multiple_of(grp_q * 128, 128), 128), :]
        row = lax.broadcasted_iota(jnp.int32, rhs.shape, 0) // seq
        return grp_q, jnp.where(row == q - grp_q * per, rhs.astype(F32), 0.0).astype(BF)

    def outer(grp_q, rhs, dst, m):
        grad = dot(qit[grp_q, m : m + m_step, :], rhs)
        dst[m : m + m_step, :] = (grad * wv[m : m + m_step, :]).astype(BF)

    def score(q, src):
        prod = dot(ei[...], src[...]) * hid[q_rows:, :].astype(F32)
        part = prod[:, :128]
        for at in range(128, width, 128):
            part = part + prod[:, at : at + 128]
        acc[q] += part.reshape(ex_count, seq // 8, 8, 128).sum(1)

    def step(q, src, dst):
        grp_q, rhs = outer_rhs(q + 1)
        outer(grp_q, rhs, dst, 0)
        score(q, src)
        outer(grp_q, rhs, dst, m_step)

    grp_q, rhs = outer_rhs(0)
    outer(grp_q, rhs, p0, 0)
    outer(grp_q, rhs, p0, m_step)

    def pair(i, carry):
        step(2 * i, p0, p1)
        step(2 * i + 1, p1, p0)
        return carry

    lax.fori_loop(0, q_count // 2 - 1, pair, 0)
    step(q_count - 2, p0, p1)
    score(q_count - 1, p1)
    out[...] = acc[...].sum(2)


def block_scores(n, q_count, seq, share, block, e_rows, idx, ei, qit, w, basis, q_own, q_oth, xs, zs, ys):
    _, rows, width = basis.shape
    ex_rows, j_rows = ei.shape
    q_rows = q_own.shape[1]
    ex_count = ex_rows // seq
    pieces = (*xs, *zs, *ys)
    flops = 2 * q_count * j_rows * width * (256 + ex_rows)
    return pl.pallas_call(
        functools.partial(score_kernel, n, q_count, seq, share, block, e_rows),
        out_shape=jax.ShapeDtypeStruct((q_count, ex_count, 128), F32),
        in_specs=[SMEM, VMEM, VMEM] + [ANY] * (4 + len(pieces)),
        out_specs=VMEM,
        scratch_shapes=[
            pltpu.VMEM((rows * n, width), BF),
            pltpu.VMEM((q_rows + ex_rows, width), BF),
            pltpu.VMEM((q_rows + ex_rows, width), BF),
            pltpu.VMEM((q_rows + ex_rows, width), BF),
            pltpu.VMEM((j_rows, width), F32),
            pltpu.VMEM((j_rows, width), BF),
            pltpu.VMEM((j_rows, width), BF),
            pltpu.VMEM((q_count, ex_count, 8, 128), F32),
            pltpu.SemaphoreType.DMA((5 + 4 * len(gather_parts(n)),)),
            pltpu.SemaphoreType.DMA(()),
        ],
        compiler_params=pltpu.CompilerParams(vmem_limit_bytes=48 * MIB),
        cost_estimate=pl.CostEstimate(flops=flops, bytes_accessed=8 * MIB, transcendentals=0),
        name="block_scores",
    )(idx, ei, qit, w, basis, q_own, q_oth, *pieces)


def sum_features(part, sub, sizes):
    half = part.shape[0] // 2
    mine = lax.dynamic_slice_in_dim(part, sub * half, half, 0)
    other = lax.dynamic_slice_in_dim(part, (1 - sub) * half, half, 0).astype(BF)
    mine = mine + swap(other, "sub").astype(F32)
    if sizes["owner"] == 2:
        total = mine + swap(mine.astype(BF), "owner").astype(F32)
    else:
        total = lax.psum(mine, "owner")
    total = total.astype(BF)
    rest = swap(total, "sub")
    return jnp.where(
        sub == 0, jnp.concatenate([total, rest], 0), jnp.concatenate([rest, total], 0)
    )


def shards(
    sizes,
    ex_acts,
    ex_grads,
    ex_mask,
    ex_ids,
    query_acts,
    query_grads,
    input_basis,
    hidden_basis,
    eigenvalues,
):
    n = sizes["dp"]
    dpi, grp, sub = (lax.axis_index(a) for a in ("dp", "groups", "sub"))
    ex_count, seq, input_cols = ex_acts.shape
    q_count, q_seq, _ = query_acts.shape
    blocks, rows, width = hidden_basis.shape
    j_rows = input_basis.shape[1]
    e_rows, q_rows = ex_count * seq, q_count * q_seq
    share = sizes["groups"] == 2 and rows % 32 == 0
    piece = rows // 2 if share else rows
    idx = jnp.stack([dpi, grp, sub]).astype(jnp.int32)

    acts = ex_acts.reshape(e_rows, input_cols)
    all_acts = whole(acts, gather(acts, n), n, dpi)
    marks = jnp.concatenate([ex_mask, ex_ids[:, None]], 1)
    marks = whole(marks, gather(marks, n), n, dpi)
    all_ids, keep = marks[:, seq], marks[:, :seq].reshape(n * e_rows, 1)

    pays, q_raw = prepare(
        idx,
        ex_grads.reshape(e_rows, blocks, width),
        query_grads.reshape(q_rows, blocks, width),
        hidden_basis,
        piece,
        share,
    )
    q_oth = swap(q_raw, "sub")
    wheres = [where for _, _, where in gather_parts(n)]
    xs, ys, zs = [], [], []
    for b in range(blocks):
        got = gather(pays[b], n)
        xs.append([pays[b], *got])
        zs.append([swap_part(x, "sub", n, where) for x, where in zip(xs[b], [None, *wheres])])
        ys.append([swap_part(x, "groups", n, where) for x, where in zip(got, wheres)] if share else [])

    q_in = sum_features(dot(query_acts.reshape(q_rows, input_cols), input_basis), sub, sizes)
    qit = jnp.transpose(q_in.reshape(q_rows // 128, 128, j_rows), (0, 2, 1))
    w = weights(eigenvalues)
    ei = sum_features(dot(all_acts, input_basis), sub, sizes) * keep.astype(BF)

    total = 0.0
    for b in range(blocks):
        total = total + block_scores(
            n, q_count, seq, share, b, e_rows, idx, ei, qit, w, hidden_basis,
            q_raw, q_oth, xs[b], zs[b], ys[b],
        )
    scores = total.sum(2)

    ex_total = all_ids.shape[0]
    onehot = (all_ids[:, None] == jnp.arange(ex_total, dtype=jnp.int32)[None, :]).astype(F32)
    placed = jnp.dot(scores, onehot, precision=lax.Precision.HIGHEST, preferred_element_type=F32)
    if sizes["owner"] == 2:
        pairs = [[(i, i ^ k) for i in range(4)] for k in (1, 2, 3)]
        placed = placed + sum(lax.ppermute(placed, ("owner", "sub"), p) for p in pairs)
    else:
        placed = lax.psum(placed, ("owner", "sub"))

    def columns(device):
        return lax.dynamic_slice_in_dim(placed, lax.rem(device, n) * ex_count, ex_count, 1)

    result = columns(dpi)
    for k in range(1, n):
        pairs = [(i, (i + k) % n) for i in range(n)]
        result = result + lax.ppermute(columns(dpi + k), "dp", pairs)
    return result


def solution(mesh):
    in_specs = (
        P(("groups", "dp"), None, ("owner", "sub")),
        P(("groups", "dp"), None, "owner", "sub"),
        P(("groups", "dp"), None),
        P(("groups", "dp")),
        P("groups", None, ("owner", "sub")),
        P("groups", None, "owner", "sub"),
        P(("owner", "sub"), "dp"),
        P("owner", "dp", "sub"),
        P("dp", "owner", "sub"),
    )
    out_specs = P("groups", "dp")
    body = functools.partial(shards, dict(mesh.shape))
    return jax.shard_map(body, mesh=mesh, in_specs=in_specs, out_specs=out_specs, check_vma=False)
```

```python
import functools

import jax
import jax.numpy as jnp
from jax import lax
from jax.experimental import pallas as pl
from jax.experimental.pallas import tpu as pltpu
from jax.sharding import PartitionSpec as P

DAMP = 0.05
BF = jnp.bfloat16
F32 = jnp.float32
MIB = 1024 * 1024
ANY = pl.BlockSpec(memory_space=pl.ANY)
VMEM = pl.BlockSpec(memory_space=pltpu.VMEM)
SMEM = pl.BlockSpec(memory_space=pltpu.SMEM)


def dot(a, b):
    return jnp.dot(a, b, preferred_element_type=F32)


def swap(x, axis):
    return lax.ppermute(x, axis, [(0, 1), (1, 0)])


def ring(x, n):
    parts = [x]
    for _ in range(n - 1):
        parts.append(lax.ppermute(parts[-1], "dp", [(i, (i + 1) % n) for i in range(n)]))
    return parts


def weight_kernel(blocks, step, lam, w, buf, sems):
    i, count = pl.program_id(0), pl.num_programs(0)
    per = count // blocks

    def copy(j, slot):
        def go(b):
            return pltpu.make_async_copy(
                lam.at[pl.ds(pl.multiple_of(lax.rem(j, per) * step, 8), step), b, :],
                buf.at[slot],
                sems.at[slot],
            )
        return go

    def start(j, slot):
        for b in range(blocks):
            pl.when(j // per == b)(lambda b=b: copy(j, slot)(b).start())

    @pl.when(i == 0)
    def _():
        start(i, 0)

    @pl.when(i + 1 < count)
    def _():
        start(i + 1, lax.rem(i + 1, 2))

    slot = lax.rem(i, 2)
    copy(i, slot)(0).wait()
    w[...] = 1.0 / (buf[slot] + DAMP)


def weights(lam):
    j_rows, blocks, width = lam.shape
    step = 320 if j_rows % 320 == 0 else j_rows
    return pl.pallas_call(
        functools.partial(weight_kernel, blocks, step),
        grid=(blocks * (j_rows // step),),
        out_shape=jax.ShapeDtypeStruct((blocks * j_rows, width), F32),
        in_specs=[ANY],
        out_specs=pl.BlockSpec((step, width), lambda i: (i, 0)),
        scratch_shapes=[pltpu.VMEM((2, step, width), F32), pltpu.SemaphoreType.DMA((2,))],
        compiler_params=pltpu.CompilerParams(vmem_limit_bytes=24 * MIB),
        cost_estimate=pl.CostEstimate(
            flops=4 * lam.size, bytes_accessed=8 * lam.size, transcendentals=0
        ),
        name="weights",
    )(lam)


def score_kernel(n, q_count, seq, first, idx, ei, qit, w, basis, q_own, q_oth, *rest):
    xs, zs, rest = rest[:n], rest[n : 2 * n], rest[2 * n :]
    out, full, tok_own, tok_oth, hid, wv, p0, p1, acc, sems, w_sem = rest
    sub = idx[0]
    chunk, all_rows, width = full.shape
    half_rows = all_rows // 2
    q_rows, e_rows = q_own.shape[1], xs[0].shape[1]
    j_rows = ei.shape[1]
    ex_count = ei.shape[0] // seq
    per = 128 // seq
    columns = chunk * width

    moves, w_moves = [], []
    for j in range(chunk):
        b = first + j
        moves.append((basis.at[j], full.at[j]))
        for own, oth, at, size in [(q_own, q_oth, 0, q_rows)] + [
            (xs[k], zs[k], q_rows + k * e_rows, e_rows) for k in range(n)
        ]:
            moves.append((own.at[b], tok_own.at[j, pl.ds(at, size), :]))
            moves.append((oth.at[b], tok_oth.at[j, pl.ds(at, size), :]))
        w_moves.append((w.at[pl.ds(b * j_rows, j_rows), :], wv.at[:, pl.ds(j * width, width)]))
    copies = [pltpu.make_async_copy(a, c, sems.at[i]) for i, (a, c) in enumerate(moves)]
    w_copies = [pltpu.make_async_copy(a, c, w_sem.at[i]) for i, (a, c) in enumerate(w_moves)]
    for copy in copies + w_copies:
        copy.start()
    acc[...] = jnp.zeros_like(acc)
    for copy in copies:
        copy.wait()
    for j in range(chunk):
        b_own = full[j, pl.ds(pl.multiple_of(sub * half_rows, 16), half_rows), :]
        b_oth = full[j, pl.ds(pl.multiple_of((1 - sub) * half_rows, 16), half_rows), :]
        rotated = dot(tok_own[j], b_own) + dot(tok_oth[j], b_oth)
        hid[:, j * width : (j + 1) * width] = rotated.astype(BF)
    for copy in w_copies:
        copy.wait()

    m_step = j_rows // 2
    tiles = [(at, min(256, columns - at)) for at in range(0, columns, 256)]

    def outer(q, dst, at, size):
        grp_q = q // per
        rhs = hid[pl.ds(pl.multiple_of(grp_q * 128, 128), 128), at : at + size]
        row = lax.broadcasted_iota(jnp.int32, rhs.shape, 0) // seq
        rhs = jnp.where(row == q - grp_q * per, rhs.astype(F32), 0.0).astype(BF)
        for m in range(0, j_rows, m_step):
            grad = dot(qit[grp_q, m : m + m_step, :], rhs)
            dst[m : m + m_step, at : at + size] = (
                grad * wv[m : m + m_step, at : at + size]
            ).astype(BF)

    def score(src, at, size):
        prod = dot(ei[...], src[:, at : at + size]) * hid[q_rows:, at : at + size].astype(F32)
        part = sum(prod[:, i : i + 128] for i in range(0, size, 128))
        return part.reshape(ex_count, seq // 8, 8, 128).sum(1)

    def step(q, src, dst):
        part = 0.0
        for at, size in tiles:
            if src is not None:
                part = part + score(src, at, size)
            if dst is not None:
                outer(q + 1, dst, at, size)
        if src is not None:
            acc[q] = part

    step(-1, None, p0)

    def pair(i, carry):
        step(2 * i, p0, p1)
        step(2 * i + 1, p1, p0)
        return carry

    lax.fori_loop(0, q_count // 2 - 1, pair, 0)
    step(q_count - 2, p0, p1)
    step(q_count - 1, p1, None)
    out[...] = acc[...].sum(2)


def chunk_scores(n, q_count, seq, first, idx, ei, qit, w, basis, q_own, q_oth, xs, zs):
    chunk, all_rows, width = basis.shape
    ex_rows, j_rows = ei.shape
    q_rows = q_own.shape[1]
    ex_count = ex_rows // seq
    tokens = pltpu.VMEM((chunk, q_rows + ex_rows, width), BF)
    flops = 2 * q_count * j_rows * chunk * width * (256 + ex_rows)
    return pl.pallas_call(
        functools.partial(score_kernel, n, q_count, seq, first),
        out_shape=jax.ShapeDtypeStruct((q_count, ex_count, 128), F32),
        in_specs=[SMEM, VMEM, VMEM] + [ANY] * (4 + 2 * n),
        out_specs=VMEM,
        scratch_shapes=[
            pltpu.VMEM((chunk, all_rows, width), BF),
            tokens,
            tokens,
            pltpu.VMEM((q_rows + ex_rows, chunk * width), BF),
            pltpu.VMEM((j_rows, chunk * width), F32),
            pltpu.VMEM((j_rows, chunk * width), BF),
            pltpu.VMEM((j_rows, chunk * width), BF),
            pltpu.VMEM((q_count, ex_count, 8, 128), F32),
            pltpu.SemaphoreType.DMA((chunk * (3 + 2 * n),)),
            pltpu.SemaphoreType.DMA((chunk,)),
        ],
        compiler_params=pltpu.CompilerParams(vmem_limit_bytes=52 * MIB),
        cost_estimate=pl.CostEstimate(flops=flops, bytes_accessed=12 * MIB, transcendentals=0),
        name="chunk_scores",
    )(idx, ei, qit, w, basis, q_own, q_oth, *xs, *zs)


def sum_features(part, sub, sizes):
    half = part.shape[0] // 2
    mine = lax.dynamic_slice_in_dim(part, sub * half, half, 0)
    other = lax.dynamic_slice_in_dim(part, (1 - sub) * half, half, 0).astype(BF)
    mine = mine + swap(other, "sub").astype(F32)
    if sizes["owner"] == 2:
        total = mine + swap(mine.astype(BF), "owner").astype(F32)
    else:
        total = lax.psum(mine, "owner")
    total = total.astype(BF)
    rest = swap(total, "sub")
    return jnp.where(
        sub == 0, jnp.concatenate([total, rest], 0), jnp.concatenate([rest, total], 0)
    )


def shards(
    sizes,
    ex_acts,
    ex_grads,
    ex_mask,
    ex_ids,
    query_acts,
    query_grads,
    input_basis,
    hidden_basis,
    eigenvalues,
):
    n = sizes["dp"]
    dpi, grp, sub = (lax.axis_index(a) for a in ("dp", "groups", "sub"))
    ex_count, seq, input_cols = ex_acts.shape
    q_count, q_seq, _ = query_acts.shape
    blocks, rows, width = hidden_basis.shape
    j_rows = input_basis.shape[1]
    e_rows, q_rows = ex_count * seq, q_count * q_seq
    share = sizes["groups"] == 2 and rows % 32 == 0
    idx = sub.astype(jnp.int32).reshape(1)

    acts = ring(ex_acts.reshape(e_rows, input_cols), n)
    keep = ex_mask.astype(BF).reshape(e_rows, 1, 1)
    e_raw = jnp.transpose(ex_grads.reshape(e_rows, blocks, width) * keep, (1, 0, 2))
    q_raw = jnp.transpose(query_grads.reshape(q_rows, blocks, width), (1, 0, 2))
    xs = ring(e_raw, n)
    zs = [swap(x, "sub") for x in xs]
    q_oth = swap(q_raw, "sub")
    all_ids = jnp.concatenate(ring(ex_ids, n))

    chunk = 2 if blocks % 2 == 0 else 1
    mine = hidden_basis
    if share:
        mine = lax.dynamic_slice_in_dim(hidden_basis, grp * (rows // 2), rows // 2, 1)
    full = [
        lax.all_gather(
            mine[b : b + chunk], ("dp", "groups") if share else "dp", axis=1, tiled=True
        )
        for b in range(0, blocks, chunk)
    ]

    q_in = sum_features(dot(query_acts.reshape(q_rows, input_cols), input_basis), sub, sizes)
    qit = jnp.transpose(q_in.reshape(q_rows // 128, 128, j_rows), (0, 2, 1))
    w = weights(eigenvalues)
    ei = sum_features(dot(jnp.concatenate(acts, 0), input_basis), sub, sizes)

    total = 0.0
    for i, basis in enumerate(full):
        total = total + chunk_scores(
            n, q_count, seq, i * chunk, idx, ei, qit, w, basis, q_raw, q_oth, xs, zs
        )
    scores = total.sum(2)

    ex_total = all_ids.shape[0]
    onehot = (all_ids[:, None] == jnp.arange(ex_total, dtype=jnp.int32)[None, :]).astype(F32)
    placed = jnp.dot(scores, onehot, precision=lax.Precision.HIGHEST, preferred_element_type=F32)
    if sizes["owner"] == 2:
        pairs = [[(i, i ^ k) for i in range(4)] for k in (1, 2, 3)]
        placed = placed + sum(lax.ppermute(placed, ("owner", "sub"), p) for p in pairs)
    else:
        placed = lax.psum(placed, ("owner", "sub"))

    def columns(device):
        return lax.dynamic_slice_in_dim(placed, lax.rem(device, n) * ex_count, ex_count, 1)

    result = columns(dpi)
    for k in range(1, n):
        pairs = [(i, (i + k) % n) for i in range(n)]
        result = result + lax.ppermute(columns(dpi + k), "dp", pairs)
    return result


def solution(mesh):
    in_specs = (
        P(("groups", "dp"), None, ("owner", "sub")),
        P(("groups", "dp"), None, "owner", "sub"),
        P(("groups", "dp"), None),
        P(("groups", "dp")),
        P("groups", None, ("owner", "sub")),
        P("groups", None, "owner", "sub"),
        P(("owner", "sub"), "dp"),
        P("owner", "dp", "sub"),
        P("dp", "owner", "sub"),
    )
    out_specs = P("groups", "dp")
    body = functools.partial(shards, dict(mesh.shape))
    return jax.shard_map(body, mesh=mesh, in_specs=in_specs, out_specs=out_specs, check_vma=False)
```

```python
import functools

import jax
import jax.numpy as jnp
from jax import lax
from jax.experimental import pallas as pl
from jax.experimental.pallas import tpu as pltpu
from jax.sharding import PartitionSpec as P

DAMP = 0.05
BF = jnp.bfloat16
F32 = jnp.float32
MIB = 1024 * 1024
ANY = pl.BlockSpec(memory_space=pl.ANY)
VMEM = pl.BlockSpec(memory_space=pltpu.VMEM)
SMEM = pl.BlockSpec(memory_space=pltpu.SMEM)


def dot(a, b):
    return jnp.dot(a, b, preferred_element_type=F32)


def swap(x, axis):
    return lax.ppermute(x, axis, [(0, 1), (1, 0)])


def step_along(x, n):
    return lax.ppermute(x, "dp", [(i, (i + 1) % n) for i in range(n)])


def ring(x, n):
    parts = [x]
    for _ in range(n - 1):
        parts.append(step_along(parts[-1], n))
    return parts


def weight_kernel(blocks, step, lam, w, buf, sems):
    i, count = pl.program_id(0), pl.num_programs(0)
    per = count // blocks

    def copy(j, slot):
        def go(b):
            return pltpu.make_async_copy(
                lam.at[pl.ds(pl.multiple_of(lax.rem(j, per) * step, 8), step), b, :],
                buf.at[slot],
                sems.at[slot],
            )
        return go

    def start(j, slot):
        for b in range(blocks):
            pl.when(j // per == b)(lambda b=b: copy(j, slot)(b).start())

    @pl.when(i == 0)
    def _():
        start(i, 0)

    @pl.when(i + 1 < count)
    def _():
        start(i + 1, lax.rem(i + 1, 2))

    slot = lax.rem(i, 2)
    copy(i, slot)(0).wait()
    w[...] = 1.0 / (buf[slot] + DAMP)


def weights(lam):
    j_rows, blocks, width = lam.shape
    step = 320 if j_rows % 320 == 0 else j_rows
    return pl.pallas_call(
        functools.partial(weight_kernel, blocks, step),
        grid=(blocks * (j_rows // step),),
        out_shape=jax.ShapeDtypeStruct((blocks * j_rows, width), F32),
        in_specs=[ANY],
        out_specs=pl.BlockSpec((step, width), lambda i: (i, 0)),
        scratch_shapes=[pltpu.VMEM((2, step, width), F32), pltpu.SemaphoreType.DMA((2,))],
        compiler_params=pltpu.CompilerParams(vmem_limit_bytes=58 * MIB),
        cost_estimate=pl.CostEstimate(
            flops=4 * lam.size, bytes_accessed=8 * lam.size, transcendentals=0
        ),
        name="weights",
    )(lam)


def score_kernel(n, q_count, seq, first, parts, idx, ei, qit, w, q_own, q_oth, *rest):
    e_own, e_oth, rest = rest[:parts], rest[parts : 2 * parts], rest[2 * parts :]
    halves, rest = rest[:-11], rest[-11:]
    out, full, tok_own, tok_oth, hid, wv, p0, p1, acc, sems, w_sem = rest
    sub, grp, dpi = idx[0], idx[1], idx[2]
    chunk, all_rows, width = full.shape
    half_rows = all_rows // 2
    q_rows, e_rows = q_own.shape[1], e_own[0].shape[1] * parts // n
    j_rows = ei.shape[1]
    ex_count = ei.shape[0] // seq
    per = 128 // seq
    columns = chunk * width

    moves, w_moves = [], []
    for j in range(chunk):
        b = first + j
        piece = all_rows // n // len(halves)
        for h, half in enumerate(halves):
            shift = (grp if h == 0 else 1 - grp) * piece if len(halves) == 2 else 0
            for k in range(n):
                to = pl.ds(pl.multiple_of(k * piece * len(halves) + shift, 16), piece)
                moves.append((half.at[j, pl.ds(k * piece, piece), :], full.at[j, to, :]))
        moves.append((q_own.at[b], tok_own.at[j, pl.ds(0, q_rows), :]))
        moves.append((q_oth.at[b], tok_oth.at[j, pl.ds(0, q_rows), :]))
        for k in range(n):
            to = pl.ds(q_rows + k * e_rows, e_rows)
            part = k if parts == n else 0
            at = 0 if parts == n else pl.multiple_of(lax.rem(dpi + n - k, n) * e_rows, 16)
            rows = pl.ds(at, e_rows)
            moves.append((e_own[part].at[j, rows, :], tok_own.at[j, to, :]))
            moves.append((e_oth[part].at[j, rows, :], tok_oth.at[j, to, :]))
        w_moves.append((w.at[pl.ds(b * j_rows, j_rows), :], wv.at[:, pl.ds(j * width, width)]))
    copies = [pltpu.make_async_copy(a, c, sems.at[i]) for i, (a, c) in enumerate(moves)]
    w_copies = [pltpu.make_async_copy(a, c, w_sem.at[i]) for i, (a, c) in enumerate(w_moves)]
    for copy in copies + w_copies:
        copy.start()
    acc[...] = jnp.zeros_like(acc)
    for copy in copies:
        copy.wait()
    for j in range(chunk):
        b_own = full[j, pl.ds(pl.multiple_of(sub * half_rows, 16), half_rows), :]
        b_oth = full[j, pl.ds(pl.multiple_of((1 - sub) * half_rows, 16), half_rows), :]
        rotated = dot(tok_own[j], b_own) + dot(tok_oth[j], b_oth)
        hid[:, j * width : (j + 1) * width] = rotated.astype(BF)
    for copy in w_copies:
        copy.wait()

    m_step = j_rows
    tiles = [(at, min(256, columns - at)) for at in range(0, columns, 256)]

    def outer(q, dst, at, size):
        grp_q = q // per
        rhs = hid[pl.ds(pl.multiple_of(grp_q * 128, 128), 128), at : at + size]
        row = lax.broadcasted_iota(jnp.int32, rhs.shape, 0) // seq
        rhs = jnp.where(row == q - grp_q * per, rhs.astype(F32), 0.0).astype(BF)
        for m in range(0, j_rows, m_step):
            grad = dot(qit[grp_q, m : m + m_step, :], rhs)
            dst[m : m + m_step, at : at + size] = (
                grad * wv[m : m + m_step, at : at + size]
            ).astype(BF)

    def score(src, at, size):
        prod = dot(ei[...], src[:, at : at + size]) * hid[q_rows:, at : at + size].astype(F32)
        part = sum(prod[:, i : i + 128] for i in range(0, size, 128))
        return part.reshape(ex_count, seq // 8, 8, 128).sum(1)

    def step(q, src, dst):
        part = 0.0
        for at, size in tiles:
            if src is not None:
                part = part + score(src, at, size)
            if dst is not None:
                outer(q + 1, dst, at, size)
        if src is not None:
            acc[q] = part

    step(-1, None, p0)

    def pair(i, carry):
        step(2 * i, p0, p1)
        step(2 * i + 1, p1, p0)
        return carry

    lax.fori_loop(0, q_count // 2 - 1, pair, 0)
    step(q_count - 2, p0, p1)
    step(q_count - 1, p1, None)
    out[...] = acc[...].sum(2)


def chunk_scores(n, q_count, seq, first, idx, ei, qit, w, q_own, q_oth, xs, zs, halves):
    chunk, _, width = halves[0].shape
    all_rows = halves[0].shape[1] * len(halves)
    ex_rows, j_rows = ei.shape
    q_rows = q_own.shape[1]
    ex_count = ex_rows // seq
    tokens = pltpu.VMEM((chunk, q_rows + ex_rows, width), BF)
    flops = 2 * q_count * j_rows * chunk * width * (256 + ex_rows)
    return pl.pallas_call(
        functools.partial(score_kernel, n, q_count, seq, first, len(xs)),
        out_shape=jax.ShapeDtypeStruct((q_count, ex_count, 128), F32),
        in_specs=[SMEM, VMEM, VMEM] + [ANY] * (3 + 2 * len(xs) + len(halves)),
        out_specs=VMEM,
        scratch_shapes=[
            pltpu.VMEM((chunk, all_rows, width), BF),
            tokens,
            tokens,
            pltpu.VMEM((q_rows + ex_rows, chunk * width), BF),
            pltpu.VMEM((j_rows, chunk * width), F32),
            pltpu.VMEM((j_rows, chunk * width), BF),
            pltpu.VMEM((j_rows, chunk * width), BF),
            pltpu.VMEM((q_count, ex_count, 8, 128), F32),
            pltpu.SemaphoreType.DMA((chunk * (2 + 2 * n + len(halves) * n),)),
            pltpu.SemaphoreType.DMA((chunk,)),
        ],
        compiler_params=pltpu.CompilerParams(vmem_limit_bytes=58 * MIB),
        cost_estimate=pl.CostEstimate(flops=flops, bytes_accessed=12 * MIB, transcendentals=0),
        name="chunk_scores",
    )(idx, ei, qit, w, q_own, q_oth, *xs, *zs, *halves)


def sum_features(part, sub, sizes):
    half = part.shape[0] // 2
    mine = lax.dynamic_slice_in_dim(part, sub * half, half, 0)
    other = lax.dynamic_slice_in_dim(part, (1 - sub) * half, half, 0).astype(BF)
    mine = mine + swap(other, "sub").astype(F32)
    if sizes["owner"] == 2:
        total = mine + swap(mine.astype(BF), "owner").astype(F32)
    else:
        total = lax.psum(mine, "owner")
    total = total.astype(BF)
    rest = swap(total, "sub")
    return jnp.where(
        sub == 0, jnp.concatenate([total, rest], 0), jnp.concatenate([rest, total], 0)
    )


def shards(
    sizes,
    ex_acts,
    ex_grads,
    ex_mask,
    ex_ids,
    query_acts,
    query_grads,
    input_basis,
    hidden_basis,
    eigenvalues,
):
    n = sizes["dp"]
    dpi, grp, sub = (lax.axis_index(a) for a in ("dp", "groups", "sub"))
    ex_count, seq, input_cols = ex_acts.shape
    q_count, q_seq, _ = query_acts.shape
    blocks, rows, width = hidden_basis.shape
    j_rows = input_basis.shape[1]
    e_rows, q_rows = ex_count * seq, q_count * q_seq
    share = sizes["groups"] == 2 and rows % 32 == 0
    idx = jnp.stack([sub, grp, dpi]).astype(jnp.int32)

    chunk = 2 if blocks % 2 == 0 else 1
    mine = hidden_basis
    if share:
        mine = lax.dynamic_slice_in_dim(hidden_basis, grp * (rows // 2), rows // 2, 1)
    lam, mine = lax.optimization_barrier((eigenvalues, mine))
    halves = [
        lax.all_gather(mine[b : b + chunk], "dp", axis=1, tiled=True)
        for b in range(0, blocks, chunk)
    ]

    keep = ex_mask.astype(BF).reshape(e_rows, 1, 1)
    e_raw = jnp.transpose(ex_grads.reshape(e_rows, blocks, width) * keep, (1, 0, 2))
    q_raw = jnp.transpose(query_grads.reshape(q_rows, blocks, width), (1, 0, 2))
    q_oth = swap(q_raw, "sub")

    w = weights(lam)
    travel = [(ex_acts.reshape(e_rows, input_cols), ex_ids, e_raw[:chunk])]
    for k in range(1, n):
        last = [step_along(x, n) for x in travel[-1]]
        if k == 1:
            *last, w = lax.optimization_barrier((*last, w))
        elif k == 2:
            *last, halves[0] = lax.optimization_barrier((*last, halves[0]))
        else:
            last = lax.optimization_barrier(last)
        travel.append(last)
    acts, ids, first = zip(*travel)
    all_ids = jnp.concatenate(ids)
    xs = [list(first)]
    zs = [[swap(x, "sub") for x in first]]

    q_in = sum_features(dot(query_acts.reshape(q_rows, input_cols), input_basis), sub, sizes)
    qit = jnp.transpose(q_in.reshape(q_rows // 128, 128, j_rows), (0, 2, 1))
    ei = sum_features(dot(jnp.concatenate(acts, 0), input_basis), sub, sizes)

    others = [swap(half, "groups") if share else None for half in halves]
    total = 0.0
    for i in range(blocks // chunk):
        if i > 0:
            later, halves[i] = lax.optimization_barrier(
                (e_raw[i * chunk : (i + 1) * chunk], halves[i])
            )
            later = lax.all_gather(later, "dp", axis=1, tiled=True)
            later, total = lax.optimization_barrier((later, total))
            xs.append([later])
            zs.append([swap(later, "sub")])
        rows_here = [halves[i], others[i]] if share else [halves[i]]
        total = total + chunk_scores(
            n, q_count, seq, i * chunk, idx, ei, qit, w, q_raw, q_oth, xs[i], zs[i], rows_here
        )
    scores = total.sum(2)

    ex_total = all_ids.shape[0]
    onehot = (all_ids[:, None] == jnp.arange(ex_total, dtype=jnp.int32)[None, :]).astype(F32)
    placed = jnp.dot(scores, onehot, precision=lax.Precision.HIGHEST, preferred_element_type=F32)
    if sizes["owner"] == 2:
        pairs = [[(i, i ^ k) for i in range(4)] for k in (1, 2, 3)]
        placed = placed + sum(lax.ppermute(placed, ("owner", "sub"), p) for p in pairs)
    else:
        placed = lax.psum(placed, ("owner", "sub"))

    def columns(device):
        return lax.dynamic_slice_in_dim(placed, lax.rem(device, n) * ex_count, ex_count, 1)

    result = columns(dpi)
    for k in range(1, n):
        pairs = [(i, (i + k) % n) for i in range(n)]
        result = result + lax.ppermute(columns(dpi + k), "dp", pairs)
    return result


def solution(mesh):
    in_specs = (
        P(("groups", "dp"), None, ("owner", "sub")),
        P(("groups", "dp"), None, "owner", "sub"),
        P(("groups", "dp"), None),
        P(("groups", "dp")),
        P("groups", None, ("owner", "sub")),
        P("groups", None, "owner", "sub"),
        P(("owner", "sub"), "dp"),
        P("owner", "dp", "sub"),
        P("dp", "owner", "sub"),
    )
    out_specs = P("groups", "dp")
    body = functools.partial(shards, dict(mesh.shape))
    return jax.shard_map(body, mesh=mesh, in_specs=in_specs, out_specs=out_specs, check_vma=False)
```

```python
import functools

import jax
import jax.numpy as jnp
from jax import lax
from jax.experimental import pallas as pl
from jax.experimental.pallas import tpu as pltpu
from jax.sharding import PartitionSpec as P

DAMP = 0.05
BF = jnp.bfloat16
F32 = jnp.float32
MIB = 1024 * 1024
ANY = pl.BlockSpec(memory_space=pl.ANY)
VMEM = pl.BlockSpec(memory_space=pltpu.VMEM)
SMEM = pl.BlockSpec(memory_space=pltpu.SMEM)


def dot(a, b):
    return jnp.dot(a, b, preferred_element_type=F32)


def swap(x, axis):
    return lax.ppermute(x, axis, [(0, 1), (1, 0)])


def step_along(x, n):
    return lax.ppermute(x, "dp", [(i, (i + 1) % n) for i in range(n)])


def ring(x, n):
    parts = [x]
    for _ in range(n - 1):
        parts.append(step_along(parts[-1], n))
    return parts


def weight_kernel(blocks, step, lam, w, buf, sems):
    i, count = pl.program_id(0), pl.num_programs(0)
    per = count // blocks

    def copy(j, slot):
        def go(b):
            return pltpu.make_async_copy(
                lam.at[pl.ds(pl.multiple_of(lax.rem(j, per) * step, 8), step), b, :],
                buf.at[slot],
                sems.at[slot],
            )
        return go

    def start(j, slot):
        for b in range(blocks):
            pl.when(j // per == b)(lambda b=b: copy(j, slot)(b).start())

    @pl.when(i == 0)
    def _():
        start(i, 0)

    @pl.when(i + 1 < count)
    def _():
        start(i + 1, lax.rem(i + 1, 2))

    slot = lax.rem(i, 2)
    copy(i, slot)(0).wait()
    w[...] = 1.0 / (buf[slot] + DAMP)


def weights(lam):
    j_rows, blocks, width = lam.shape
    step = 320 if j_rows % 320 == 0 else j_rows
    return pl.pallas_call(
        functools.partial(weight_kernel, blocks, step),
        grid=(blocks * (j_rows // step),),
        out_shape=jax.ShapeDtypeStruct((blocks * j_rows, width), F32),
        in_specs=[ANY],
        out_specs=pl.BlockSpec((step, width), lambda i: (i, 0)),
        scratch_shapes=[pltpu.VMEM((2, step, width), F32), pltpu.SemaphoreType.DMA((2,))],
        compiler_params=pltpu.CompilerParams(vmem_limit_bytes=58 * MIB),
        cost_estimate=pl.CostEstimate(
            flops=4 * lam.size, bytes_accessed=8 * lam.size, transcendentals=0
        ),
        name="weights",
    )(lam)


def score_kernel(n, q_count, seq, first, share, idx, ei, qit, w, q_own, q_oth, *rest):
    e_own, e_oth, rest = rest[:n], rest[n : 2 * n], rest[2 * n :]
    gathered, rest = rest[:-11], rest[-11:]
    out, full, tok_own, tok_oth, hid, wv, p0, p1, acc, sems, w_sem = rest
    sub, grp = idx[0], idx[1]
    chunk, all_rows, width = full.shape
    half_rows = all_rows // 2
    q_rows, e_rows = q_own.shape[1], e_own[0].shape[1]
    j_rows = ei.shape[1]
    ex_count = ei.shape[0] // seq
    per = 128 // seq
    columns = chunk * width

    moves, w_moves = [], []
    for j in range(chunk):
        b = first + j
        if share:
            piece = all_rows // n // 2
            for half, side in zip(gathered, (grp, 1 - grp)):
                for k in range(n):
                    to = pl.ds(pl.multiple_of((2 * k + side) * piece, 16), piece)
                    moves.append((half.at[j, pl.ds(k * piece, piece), :], full.at[j, to, :]))
        else:
            moves.append((gathered[j].at[0], full.at[j]))
        moves.append((q_own.at[b], tok_own.at[j, pl.ds(0, q_rows), :]))
        moves.append((q_oth.at[b], tok_oth.at[j, pl.ds(0, q_rows), :]))
        for k in range(n):
            to = pl.ds(q_rows + k * e_rows, e_rows)
            moves.append((e_own[k].at[b], tok_own.at[j, to, :]))
            moves.append((e_oth[k].at[b], tok_oth.at[j, to, :]))
        w_moves.append((w.at[pl.ds(b * j_rows, j_rows), :], wv.at[:, pl.ds(j * width, width)]))
    copies = [pltpu.make_async_copy(a, c, sems.at[i]) for i, (a, c) in enumerate(moves)]
    w_copies = [pltpu.make_async_copy(a, c, w_sem.at[i]) for i, (a, c) in enumerate(w_moves)]
    for copy in copies + w_copies:
        copy.start()
    acc[...] = jnp.zeros_like(acc)
    for copy in copies:
        copy.wait()
    for j in range(chunk):
        b_own = full[j, pl.ds(pl.multiple_of(sub * half_rows, 16), half_rows), :]
        b_oth = full[j, pl.ds(pl.multiple_of((1 - sub) * half_rows, 16), half_rows), :]
        rotated = dot(tok_own[j], b_own) + dot(tok_oth[j], b_oth)
        hid[:, j * width : (j + 1) * width] = rotated.astype(BF)
    for copy in w_copies:
        copy.wait()

    m_step = j_rows
    tiles = [(at, min(256, columns - at)) for at in range(0, columns, 256)]

    def outer(q, dst, at, size):
        grp_q = q // per
        rhs = hid[pl.ds(pl.multiple_of(grp_q * 128, 128), 128), at : at + size]
        row = lax.broadcasted_iota(jnp.int32, rhs.shape, 0) // seq
        rhs = jnp.where(row == q - grp_q * per, rhs.astype(F32), 0.0).astype(BF)
        for m in range(0, j_rows, m_step):
            grad = dot(qit[grp_q, m : m + m_step, :], rhs)
            dst[m : m + m_step, at : at + size] = (
                grad * wv[m : m + m_step, at : at + size]
            ).astype(BF)

    def score(src, at, size):
        prod = dot(ei[...], src[:, at : at + size]) * hid[q_rows:, at : at + size].astype(F32)
        part = sum(prod[:, i : i + 128] for i in range(0, size, 128))
        return part.reshape(ex_count, seq // 8, 8, 128).sum(1)

    def step(q, src, dst):
        part = 0.0
        for at, size in tiles:
            if src is not None:
                part = part + score(src, at, size)
            if dst is not None:
                outer(q + 1, dst, at, size)
        if src is not None:
            acc[q] = part

    step(-1, None, p0)

    def pair(i, carry):
        step(2 * i, p0, p1)
        step(2 * i + 1, p1, p0)
        return carry

    lax.fori_loop(0, q_count // 2 - 1, pair, 0)
    step(q_count - 2, p0, p1)
    step(q_count - 1, p1, None)
    out[...] = acc[...].sum(2)


def chunk_scores(n, q_count, seq, first, share, idx, ei, qit, w, q_own, q_oth, xs, zs, gathered):
    chunk, all_rows, width = gathered[0].shape
    if share:
        all_rows *= 2
    else:
        chunk = len(gathered)
    ex_rows, j_rows = ei.shape
    q_rows = q_own.shape[1]
    ex_count = ex_rows // seq
    tokens = pltpu.VMEM((chunk, q_rows + ex_rows, width), BF)
    flops = 2 * q_count * j_rows * chunk * width * (256 + ex_rows)
    return pl.pallas_call(
        functools.partial(score_kernel, n, q_count, seq, first, share),
        out_shape=jax.ShapeDtypeStruct((q_count, ex_count, 128), F32),
        in_specs=[SMEM, VMEM, VMEM] + [ANY] * (3 + 2 * n + len(gathered)),
        out_specs=VMEM,
        scratch_shapes=[
            pltpu.VMEM((chunk, all_rows, width), BF),
            tokens,
            tokens,
            pltpu.VMEM((q_rows + ex_rows, chunk * width), BF),
            pltpu.VMEM((j_rows, chunk * width), F32),
            pltpu.VMEM((j_rows, chunk * width), BF),
            pltpu.VMEM((j_rows, chunk * width), BF),
            pltpu.VMEM((q_count, ex_count, 8, 128), F32),
            pltpu.SemaphoreType.DMA((chunk * (2 + 2 * n + 2 * n),)),
            pltpu.SemaphoreType.DMA((chunk,)),
        ],
        compiler_params=pltpu.CompilerParams(vmem_limit_bytes=58 * MIB),
        cost_estimate=pl.CostEstimate(flops=flops, bytes_accessed=12 * MIB, transcendentals=0),
        name="chunk_scores",
    )(idx, ei, qit, w, q_own, q_oth, *xs, *zs, *gathered)


def sum_cores(part, sub):
    half = part.shape[0] // 2
    mine = lax.dynamic_slice_in_dim(part, sub * half, half, 0)
    other = lax.dynamic_slice_in_dim(part, (1 - sub) * half, half, 0).astype(BF)
    return mine + swap(other, "sub").astype(F32)


def sum_owners(mine, sizes):
    if sizes["owner"] == 2:
        total = mine + swap(mine.astype(BF), "owner").astype(F32)
    else:
        total = lax.psum(mine, "owner")
    return total.astype(BF)


def both_halves(total, rest, sub):
    return jnp.where(
        sub == 0, jnp.concatenate([total, rest], 0), jnp.concatenate([rest, total], 0)
    )


def shards(
    sizes,
    ex_acts,
    ex_grads,
    ex_mask,
    ex_ids,
    query_acts,
    query_grads,
    input_basis,
    hidden_basis,
    eigenvalues,
):
    n = sizes["dp"]
    dpi, grp, sub = (lax.axis_index(a) for a in ("dp", "groups", "sub"))
    ex_count, seq, input_cols = ex_acts.shape
    q_count, q_seq, _ = query_acts.shape
    blocks, rows, width = hidden_basis.shape
    j_rows = input_basis.shape[1]
    e_rows, q_rows = ex_count * seq, q_count * q_seq
    share = sizes["groups"] == 2 and rows % 32 == 0
    idx = jnp.stack([sub, grp, dpi]).astype(jnp.int32)

    tie = lax.optimization_barrier

    chunk = 2 if blocks % 2 == 0 else 1
    share = share and chunk < blocks
    lead = chunk if share else 0
    mine = hidden_basis[:lead]
    if share:
        mine = lax.dynamic_slice_in_dim(mine, grp * (rows // 2), rows // 2, 1)
        mine = lax.all_gather(mine, "dp", axis=1, tiled=True)
    later = [
        lax.all_gather(hidden_basis[b : b + 1], "dp", axis=1, tiled=True)
        for b in range(lead, blocks)
    ]

    keep = ex_mask.astype(BF).reshape(e_rows, 1, 1)
    e_raw = jnp.transpose(ex_grads.reshape(e_rows, blocks, width) * keep, (1, 0, 2))
    q_raw = jnp.transpose(query_grads.reshape(q_rows, blocks, width), (1, 0, 2))

    acts, ids = [ex_acts.reshape(e_rows, input_cols)], [ex_ids]
    q_in = dot(query_acts.reshape(q_rows, input_cols), input_basis)
    q_rest = None
    for k in range(1, n):
        act, num = step_along(acts[-1], n), step_along(ids[-1], n)
        if k == 1:
            act, num, q_in = tie((act, num, sum_cores(q_in, sub)))
        elif k == 2:
            act, num, q_in = tie((act, num, sum_owners(q_in, sizes)))
        elif k == 3:
            q_rest = swap(q_in, "sub")
            act, num, q_rest, e_raw, q_raw, mine = tie((act, num, q_rest, e_raw, q_raw, mine))
        else:
            act, num = tie((act, num))
        acts.append(act)
        ids.append(num)
    all_ids = jnp.concatenate(ids)
    q_in = both_halves(q_in, q_rest, sub)
    qit = jnp.transpose(q_in.reshape(q_rows // 128, 128, j_rows), (0, 2, 1))

    xs, ei, ei_rest, w = [e_raw], dot(jnp.concatenate(acts, 0), input_basis), None, None
    for k in range(1, n):
        raw = step_along(xs[-1], n)
        if k == 1:
            raw, ei = tie((raw, sum_cores(ei, sub)))
        elif k == 2:
            raw, ei, w = tie((raw, sum_owners(ei, sizes), weights(eigenvalues)))
        elif k == 3:
            raw, ei_rest = tie((raw, swap(ei, "sub")))
        xs.append(raw)
    ei = both_halves(ei, ei_rest, sub)
    q_oth = swap(q_raw, "sub")
    zs = [swap(x, "sub") for x in xs]

    total = 0.0
    for first in range(0, blocks, chunk):
        if first < lead:
            gathered = [mine, swap(mine, "groups")]
            gathered[1], later[0] = tie((gathered[1], later[0]))
        else:
            gathered = later[first - lead : first - lead + chunk]
        total = total + chunk_scores(
            n, q_count, seq, first, first < lead, idx, ei, qit, w, q_raw, q_oth, xs, zs, gathered
        )
    scores = total.sum(2)

    ex_total = all_ids.shape[0]
    onehot = (all_ids[:, None] == jnp.arange(ex_total, dtype=jnp.int32)[None, :]).astype(F32)
    placed = jnp.dot(scores, onehot, precision=lax.Precision.HIGHEST, preferred_element_type=F32)
    if sizes["owner"] == 2:
        pairs = [[(i, i ^ k) for i in range(4)] for k in (1, 2, 3)]
        placed = placed + sum(lax.ppermute(placed, ("owner", "sub"), p) for p in pairs)
    else:
        placed = lax.psum(placed, ("owner", "sub"))

    def columns(device):
        return lax.dynamic_slice_in_dim(placed, lax.rem(device, n) * ex_count, ex_count, 1)

    result = columns(dpi)
    for k in range(1, n):
        pairs = [(i, (i + k) % n) for i in range(n)]
        result = result + lax.ppermute(columns(dpi + k), "dp", pairs)
    return result


def solution(mesh):
    in_specs = (
        P(("groups", "dp"), None, ("owner", "sub")),
        P(("groups", "dp"), None, "owner", "sub"),
        P(("groups", "dp"), None),
        P(("groups", "dp")),
        P("groups", None, ("owner", "sub")),
        P("groups", None, "owner", "sub"),
        P(("owner", "sub"), "dp"),
        P("owner", "dp", "sub"),
        P("dp", "owner", "sub"),
    )
    out_specs = P("groups", "dp")
    body = functools.partial(shards, dict(mesh.shape))
    return jax.shard_map(body, mesh=mesh, in_specs=in_specs, out_specs=out_specs, check_vma=False)
```

```python
import functools

import jax
import jax.numpy as jnp
from jax import lax
from jax.experimental import pallas as pl
from jax.experimental.pallas import tpu as pltpu
from jax.sharding import PartitionSpec as P

DAMP = 0.05
BF = jnp.bfloat16
F32 = jnp.float32
MIB = 1024 * 1024
ANY = pl.BlockSpec(memory_space=pl.ANY)
VMEM = pl.BlockSpec(memory_space=pltpu.VMEM)
SMEM = pl.BlockSpec(memory_space=pltpu.SMEM)


def dot(a, b):
    return jnp.dot(a, b, preferred_element_type=F32)


def swap(x, axis):
    return lax.ppermute(x, axis, [(0, 1), (1, 0)])


def step_along(x, n):
    return lax.ppermute(x, "dp", [(i, (i + 1) % n) for i in range(n)])


def ring(x, n):
    parts = [x]
    for _ in range(n - 1):
        parts.append(step_along(parts[-1], n))
    return parts


def weight_kernel(blocks, step, lam, w, buf, sems):
    i, count = pl.program_id(0), pl.num_programs(0)
    per = count // blocks

    def copy(j, slot):
        def go(b):
            return pltpu.make_async_copy(
                lam.at[pl.ds(pl.multiple_of(lax.rem(j, per) * step, 8), step), b, :],
                buf.at[slot],
                sems.at[slot],
            )
        return go

    def start(j, slot):
        for b in range(blocks):
            pl.when(j // per == b)(lambda b=b: copy(j, slot)(b).start())

    @pl.when(i == 0)
    def _():
        start(i, 0)

    @pl.when(i + 1 < count)
    def _():
        start(i + 1, lax.rem(i + 1, 2))

    slot = lax.rem(i, 2)
    copy(i, slot)(0).wait()
    w[...] = 1.0 / (buf[slot] + DAMP)


def weights(lam):
    j_rows, blocks, width = lam.shape
    step = 320 if j_rows % 320 == 0 else j_rows
    return pl.pallas_call(
        functools.partial(weight_kernel, blocks, step),
        grid=(blocks * (j_rows // step),),
        out_shape=jax.ShapeDtypeStruct((blocks * j_rows, width), F32),
        in_specs=[ANY],
        out_specs=pl.BlockSpec((step, width), lambda i: (i, 0)),
        scratch_shapes=[pltpu.VMEM((2, step, width), F32), pltpu.SemaphoreType.DMA((2,))],
        compiler_params=pltpu.CompilerParams(vmem_limit_bytes=58 * MIB),
        cost_estimate=pl.CostEstimate(
            flops=4 * lam.size, bytes_accessed=8 * lam.size, transcendentals=0
        ),
        name="weights",
    )(lam)


def score_kernel(n, q_count, seq, first, idx, ei, qit, w, basis, q_own, q_oth, *rest):
    xs, zs, rest = rest[:n], rest[n : 2 * n], rest[2 * n :]
    out, full, tok_own, tok_oth, hid, wv, p0, p1, acc, sems, w_sem = rest
    sub = idx[0]
    chunk, all_rows, width = full.shape
    half_rows = all_rows // 2
    q_rows, e_rows = q_own.shape[1], xs[0].shape[1]
    j_rows = ei.shape[1]
    ex_count = ei.shape[0] // seq
    per = 128 // seq
    columns = chunk * width

    moves, w_moves = [], []
    for j in range(chunk):
        b = first + j
        moves.append((basis.at[j], full.at[j]))
        for own, oth, at, size in [(q_own, q_oth, 0, q_rows)] + [
            (xs[k], zs[k], q_rows + k * e_rows, e_rows) for k in range(n)
        ]:
            moves.append((own.at[b], tok_own.at[j, pl.ds(at, size), :]))
            moves.append((oth.at[b], tok_oth.at[j, pl.ds(at, size), :]))
        w_moves.append((w.at[pl.ds(b * j_rows, j_rows), :], wv.at[:, pl.ds(j * width, width)]))
    copies = [pltpu.make_async_copy(a, c, sems.at[i]) for i, (a, c) in enumerate(moves)]
    w_copies = [pltpu.make_async_copy(a, c, w_sem.at[i]) for i, (a, c) in enumerate(w_moves)]
    for copy in copies + w_copies:
        copy.start()
    acc[...] = jnp.zeros_like(acc)
    for copy in copies:
        copy.wait()
    for j in range(chunk):
        b_own = full[j, pl.ds(pl.multiple_of(sub * half_rows, 16), half_rows), :]
        b_oth = full[j, pl.ds(pl.multiple_of((1 - sub) * half_rows, 16), half_rows), :]
        rotated = dot(tok_own[j], b_own) + dot(tok_oth[j], b_oth)
        hid[:, j * width : (j + 1) * width] = rotated.astype(BF)
    for copy in w_copies:
        copy.wait()

    m_step = j_rows // 2
    tiles = [(at, min(256, columns - at)) for at in range(0, columns, 256)]

    def outer(q, dst, at, size):
        grp_q = q // per
        rhs = hid[pl.ds(pl.multiple_of(grp_q * 128, 128), 128), at : at + size]
        row = lax.broadcasted_iota(jnp.int32, rhs.shape, 0) // seq
        rhs = jnp.where(row == q - grp_q * per, rhs.astype(F32), 0.0).astype(BF)
        for m in range(0, j_rows, m_step):
            grad = dot(qit[grp_q, m : m + m_step, :], rhs)
            dst[m : m + m_step, at : at + size] = (
                grad * wv[m : m + m_step, at : at + size]
            ).astype(BF)

    def score(src, at, size):
        prod = dot(ei[...], src[:, at : at + size]) * hid[q_rows:, at : at + size].astype(F32)
        part = sum(prod[:, i : i + 128] for i in range(0, size, 128))
        return part.reshape(ex_count, seq // 8, 8, 128).sum(1)

    def step(q, src, dst):
        part = 0.0
        for at, size in tiles:
            if src is not None:
                part = part + score(src, at, size)
            if dst is not None:
                outer(q + 1, dst, at, size)
        if src is not None:
            acc[q] = part

    step(-1, None, p0)

    def pair(i, carry):
        step(2 * i, p0, p1)
        step(2 * i + 1, p1, p0)
        return carry

    lax.fori_loop(0, q_count // 2 - 1, pair, 0)
    step(q_count - 2, p0, p1)
    step(q_count - 1, p1, None)
    out[...] = acc[...].sum(2)


def chunk_scores(n, q_count, seq, first, idx, ei, qit, w, basis, q_own, q_oth, xs, zs):
    chunk, all_rows, width = basis.shape
    ex_rows, j_rows = ei.shape
    q_rows = q_own.shape[1]
    ex_count = ex_rows // seq
    tokens = pltpu.VMEM((chunk, q_rows + ex_rows, width), BF)
    flops = 2 * q_count * j_rows * chunk * width * (256 + ex_rows)
    return pl.pallas_call(
        functools.partial(score_kernel, n, q_count, seq, first),
        out_shape=jax.ShapeDtypeStruct((q_count, ex_count, 128), F32),
        in_specs=[SMEM, VMEM, VMEM] + [ANY] * (4 + 2 * n),
        out_specs=VMEM,
        scratch_shapes=[
            pltpu.VMEM((chunk, all_rows, width), BF),
            tokens,
            tokens,
            pltpu.VMEM((q_rows + ex_rows, chunk * width), BF),
            pltpu.VMEM((j_rows, chunk * width), F32),
            pltpu.VMEM((j_rows, chunk * width), BF),
            pltpu.VMEM((j_rows, chunk * width), BF),
            pltpu.VMEM((q_count, ex_count, 8, 128), F32),
            pltpu.SemaphoreType.DMA((chunk * (3 + 2 * n),)),
            pltpu.SemaphoreType.DMA((chunk,)),
        ],
        compiler_params=pltpu.CompilerParams(vmem_limit_bytes=58 * MIB),
        cost_estimate=pl.CostEstimate(flops=flops, bytes_accessed=12 * MIB, transcendentals=0),
        name="chunk_scores",
    )(idx, ei, qit, w, basis, q_own, q_oth, *xs, *zs)


def sum_features(part, sub, sizes):
    half = part.shape[0] // 2
    mine = lax.dynamic_slice_in_dim(part, sub * half, half, 0)
    other = lax.dynamic_slice_in_dim(part, (1 - sub) * half, half, 0).astype(BF)
    mine = mine + swap(other, "sub").astype(F32)
    if sizes["owner"] == 2:
        total = mine + swap(mine.astype(BF), "owner").astype(F32)
    else:
        total = lax.psum(mine, "owner")
    total = total.astype(BF)
    rest = swap(total, "sub")
    return jnp.where(
        sub == 0, jnp.concatenate([total, rest], 0), jnp.concatenate([rest, total], 0)
    )


def shards(
    sizes,
    ex_acts,
    ex_grads,
    ex_mask,
    ex_ids,
    query_acts,
    query_grads,
    input_basis,
    hidden_basis,
    eigenvalues,
):
    n = sizes["dp"]
    dpi, grp, sub = (lax.axis_index(a) for a in ("dp", "groups", "sub"))
    ex_count, seq, input_cols = ex_acts.shape
    q_count, q_seq, _ = query_acts.shape
    blocks, rows, width = hidden_basis.shape
    j_rows = input_basis.shape[1]
    e_rows, q_rows = ex_count * seq, q_count * q_seq
    share = sizes["groups"] == 2 and rows % 32 == 0
    idx = sub.astype(jnp.int32).reshape(1)

    chunk = 2 if blocks % 2 == 0 else 1
    mine = hidden_basis
    if share:
        mine = lax.dynamic_slice_in_dim(hidden_basis, grp * (rows // 2), rows // 2, 1)
    mine = [mine[b : b + chunk] for b in range(0, blocks, chunk)]
    acts, *mine = lax.optimization_barrier((ex_acts.reshape(e_rows, input_cols), *mine))
    full = [
        lax.all_gather(part, ("dp", "groups") if share else "dp", axis=1, tiled=True)
        for part in mine
    ]

    w = weights(eigenvalues)
    acts, ids = [acts], [ex_ids]
    for k in range(1, n):
        last = step_along(acts[-1], n), step_along(ids[-1], n)
        if k == 2:
            *last, w = lax.optimization_barrier((*last, w))
        else:
            last = lax.optimization_barrier(last)
        acts.append(last[0])
        ids.append(last[1])
    all_ids = jnp.concatenate(ids)

    keep = ex_mask.astype(BF).reshape(e_rows, 1, 1)
    e_raw = jnp.transpose(ex_grads.reshape(e_rows, blocks, width) * keep, (1, 0, 2))
    q_raw = jnp.transpose(query_grads.reshape(q_rows, blocks, width), (1, 0, 2))
    xs = ring(e_raw, n)
    zs = [swap(x, "sub") for x in xs]
    q_oth = swap(q_raw, "sub")

    q_in = sum_features(dot(query_acts.reshape(q_rows, input_cols), input_basis), sub, sizes)
    qit = jnp.transpose(q_in.reshape(q_rows // 128, 128, j_rows), (0, 2, 1))
    ei = sum_features(dot(jnp.concatenate(acts, 0), input_basis), sub, sizes)

    total = 0.0
    for i, basis in enumerate(full):
        total = total + chunk_scores(
            n, q_count, seq, i * chunk, idx, ei, qit, w, basis, q_raw, q_oth, xs, zs
        )
    scores = total.sum(2)

    ex_total = all_ids.shape[0]
    onehot = (all_ids[:, None] == jnp.arange(ex_total, dtype=jnp.int32)[None, :]).astype(F32)
    placed = jnp.dot(scores, onehot, precision=lax.Precision.HIGHEST, preferred_element_type=F32)
    if sizes["owner"] == 2:
        pairs = [[(i, i ^ k) for i in range(4)] for k in (1, 2, 3)]
        placed = placed + sum(lax.ppermute(placed, ("owner", "sub"), p) for p in pairs)
    else:
        placed = lax.psum(placed, ("owner", "sub"))

    def columns(device):
        return lax.dynamic_slice_in_dim(placed, lax.rem(device, n) * ex_count, ex_count, 1)

    result = columns(dpi)
    for k in range(1, n):
        pairs = [(i, (i + k) % n) for i in range(n)]
        result = result + lax.ppermute(columns(dpi + k), "dp", pairs)
    return result


def solution(mesh):
    in_specs = (
        P(("groups", "dp"), None, ("owner", "sub")),
        P(("groups", "dp"), None, "owner", "sub"),
        P(("groups", "dp"), None),
        P(("groups", "dp")),
        P("groups", None, ("owner", "sub")),
        P("groups", None, "owner", "sub"),
        P(("owner", "sub"), "dp"),
        P("owner", "dp", "sub"),
        P("dp", "owner", "sub"),
    )
    out_specs = P("groups", "dp")
    body = functools.partial(shards, dict(mesh.shape))
    return jax.shard_map(body, mesh=mesh, in_specs=in_specs, out_specs=out_specs, check_vma=False)
```

```python
import functools

import jax
import jax.numpy as jnp
from jax import lax
from jax.experimental import pallas as pl
from jax.experimental.pallas import tpu as pltpu
from jax.sharding import PartitionSpec as P

DAMP = 0.05
BF = jnp.bfloat16
F32 = jnp.float32
MIB = 1024 * 1024
ANY = pl.BlockSpec(memory_space=pl.ANY)
VMEM = pl.BlockSpec(memory_space=pltpu.VMEM)
SMEM = pl.BlockSpec(memory_space=pltpu.SMEM)


def dot(a, b):
    return jnp.dot(a, b, preferred_element_type=F32)


def swap(x, axis):
    return lax.ppermute(x, axis, [(0, 1), (1, 0)])


def step_along(x, n):
    return lax.ppermute(x, "dp", [(i, (i + 1) % n) for i in range(n)])


def ring(x, n):
    parts = [x]
    for _ in range(n - 1):
        parts.append(step_along(parts[-1], n))
    return parts


def weight_kernel(blocks, step, lam, w, buf, sems):
    i, count = pl.program_id(0), pl.num_programs(0)
    per = count // blocks

    def copy(j, slot):
        def go(b):
            return pltpu.make_async_copy(
                lam.at[pl.ds(pl.multiple_of(lax.rem(j, per) * step, 8), step), b, :],
                buf.at[slot],
                sems.at[slot],
            )
        return go

    def start(j, slot):
        for b in range(blocks):
            pl.when(j // per == b)(lambda b=b: copy(j, slot)(b).start())

    @pl.when(i == 0)
    def _():
        start(i, 0)

    @pl.when(i + 1 < count)
    def _():
        start(i + 1, lax.rem(i + 1, 2))

    slot = lax.rem(i, 2)
    copy(i, slot)(0).wait()
    w[...] = 1.0 / (buf[slot] + DAMP)


def weights(lam):
    j_rows, blocks, width = lam.shape
    step = 320 if j_rows % 320 == 0 else j_rows
    return pl.pallas_call(
        functools.partial(weight_kernel, blocks, step),
        grid=(blocks * (j_rows // step),),
        out_shape=jax.ShapeDtypeStruct((blocks * j_rows, width), F32),
        in_specs=[ANY],
        out_specs=pl.BlockSpec((step, width), lambda i: (i, 0)),
        scratch_shapes=[pltpu.VMEM((2, step, width), F32), pltpu.SemaphoreType.DMA((2,))],
        compiler_params=pltpu.CompilerParams(vmem_limit_bytes=58 * MIB),
        cost_estimate=pl.CostEstimate(
            flops=4 * lam.size, bytes_accessed=8 * lam.size, transcendentals=0
        ),
        name="weights",
    )(lam)


def score_kernel(n, q_count, seq, first, idx, ei, qit, w, basis, q_own, q_oth, *rest):
    xs, zs, rest = rest[:n], rest[n : 2 * n], rest[2 * n :]
    out, full, tok_own, tok_oth, hid, wv, p0, p1, acc, sems, w_sem = rest
    sub = idx[0]
    chunk, all_rows, width = full.shape
    half_rows = all_rows // 2
    q_rows, e_rows = q_own.shape[1], xs[0].shape[1]
    j_rows = ei.shape[1]
    ex_count = ei.shape[0] // seq
    per = 128 // seq
    columns = chunk * width

    moves, w_moves = [], []
    for j in range(chunk):
        b = first + j
        moves.append((basis.at[j], full.at[j]))
        for own, oth, at, size in [(q_own, q_oth, 0, q_rows)] + [
            (xs[k], zs[k], q_rows + k * e_rows, e_rows) for k in range(n)
        ]:
            moves.append((own.at[b], tok_own.at[j, pl.ds(at, size), :]))
            moves.append((oth.at[b], tok_oth.at[j, pl.ds(at, size), :]))
        w_moves.append((w.at[pl.ds(b * j_rows, j_rows), :], wv.at[:, pl.ds(j * width, width)]))
    copies = [pltpu.make_async_copy(a, c, sems.at[i]) for i, (a, c) in enumerate(moves)]
    w_copies = [pltpu.make_async_copy(a, c, w_sem.at[i]) for i, (a, c) in enumerate(w_moves)]
    for copy in copies + w_copies:
        copy.start()
    acc[...] = jnp.zeros_like(acc)
    for copy in copies:
        copy.wait()
    for j in range(chunk):
        b_own = full[j, pl.ds(pl.multiple_of(sub * half_rows, 16), half_rows), :]
        b_oth = full[j, pl.ds(pl.multiple_of((1 - sub) * half_rows, 16), half_rows), :]
        rotated = dot(tok_own[j], b_own) + dot(tok_oth[j], b_oth)
        hid[:, j * width : (j + 1) * width] = rotated.astype(BF)
    for copy in w_copies:
        copy.wait()

    m_step = j_rows // 2
    tiles = [(at, min(256, columns - at)) for at in range(0, columns, 256)]

    def outer(q, dst, at, size):
        grp_q = q // per
        rhs = hid[pl.ds(pl.multiple_of(grp_q * 128, 128), 128), at : at + size]
        row = lax.broadcasted_iota(jnp.int32, rhs.shape, 0) // seq
        rhs = jnp.where(row == q - grp_q * per, rhs.astype(F32), 0.0).astype(BF)
        for m in range(0, j_rows, m_step):
            grad = dot(qit[grp_q, m : m + m_step, :], rhs)
            dst[m : m + m_step, at : at + size] = (
                grad * wv[m : m + m_step, at : at + size]
            ).astype(BF)

    def score(src, at, size):
        prod = dot(ei[...], src[:, at : at + size]) * hid[q_rows:, at : at + size].astype(F32)
        part = sum(prod[:, i : i + 128] for i in range(0, size, 128))
        return part.reshape(ex_count, seq // 8, 8, 128).sum(1)

    def step(q, src, dst):
        part = 0.0
        for at, size in tiles:
            if src is not None:
                part = part + score(src, at, size)
            if dst is not None:
                outer(q + 1, dst, at, size)
        if src is not None:
            acc[q] = part

    step(-1, None, p0)

    def pair(i, carry):
        step(2 * i, p0, p1)
        step(2 * i + 1, p1, p0)
        return carry

    lax.fori_loop(0, q_count // 2 - 1, pair, 0)
    step(q_count - 2, p0, p1)
    step(q_count - 1, p1, None)
    out[...] = acc[...].sum(2)


def chunk_scores(n, q_count, seq, first, idx, ei, qit, w, basis, q_own, q_oth, xs, zs):
    chunk, all_rows, width = basis.shape
    ex_rows, j_rows = ei.shape
    q_rows = q_own.shape[1]
    ex_count = ex_rows // seq
    tokens = pltpu.VMEM((chunk, q_rows + ex_rows, width), BF)
    flops = 2 * q_count * j_rows * chunk * width * (256 + ex_rows)
    return pl.pallas_call(
        functools.partial(score_kernel, n, q_count, seq, first),
        out_shape=jax.ShapeDtypeStruct((q_count, ex_count, 128), F32),
        in_specs=[SMEM, VMEM, VMEM] + [ANY] * (4 + 2 * n),
        out_specs=VMEM,
        scratch_shapes=[
            pltpu.VMEM((chunk, all_rows, width), BF),
            tokens,
            tokens,
            pltpu.VMEM((q_rows + ex_rows, chunk * width), BF),
            pltpu.VMEM((j_rows, chunk * width), F32),
            pltpu.VMEM((j_rows, chunk * width), BF),
            pltpu.VMEM((j_rows, chunk * width), BF),
            pltpu.VMEM((q_count, ex_count, 8, 128), F32),
            pltpu.SemaphoreType.DMA((chunk * (3 + 2 * n),)),
            pltpu.SemaphoreType.DMA((chunk,)),
        ],
        compiler_params=pltpu.CompilerParams(vmem_limit_bytes=58 * MIB),
        cost_estimate=pl.CostEstimate(flops=flops, bytes_accessed=12 * MIB, transcendentals=0),
        name="chunk_scores",
    )(idx, ei, qit, w, basis, q_own, q_oth, *xs, *zs)


def sum_features(part, sub, sizes):
    half = part.shape[0] // 2
    mine = lax.dynamic_slice_in_dim(part, sub * half, half, 0)
    other = lax.dynamic_slice_in_dim(part, (1 - sub) * half, half, 0).astype(BF)
    mine = mine + swap(other, "sub").astype(F32)
    if sizes["owner"] == 2:
        total = mine + swap(mine.astype(BF), "owner").astype(F32)
    else:
        total = lax.psum(mine, "owner")
    total = total.astype(BF)
    rest = swap(total, "sub")
    return jnp.where(
        sub == 0, jnp.concatenate([total, rest], 0), jnp.concatenate([rest, total], 0)
    )


def shards(
    sizes,
    ex_acts,
    ex_grads,
    ex_mask,
    ex_ids,
    query_acts,
    query_grads,
    input_basis,
    hidden_basis,
    eigenvalues,
):
    n = sizes["dp"]
    dpi, grp, sub = (lax.axis_index(a) for a in ("dp", "groups", "sub"))
    ex_count, seq, input_cols = ex_acts.shape
    q_count, q_seq, _ = query_acts.shape
    blocks, rows, width = hidden_basis.shape
    j_rows = input_basis.shape[1]
    e_rows, q_rows = ex_count * seq, q_count * q_seq
    share = sizes["groups"] == 2 and rows % 32 == 0
    idx = sub.astype(jnp.int32).reshape(1)

    chunk = 2 if blocks % 2 == 0 else 1
    mine = hidden_basis
    if share:
        mine = lax.dynamic_slice_in_dim(hidden_basis, grp * (rows // 2), rows // 2, 1)
    mine = [mine[b : b + chunk] for b in range(0, blocks, chunk)]
    acts, *mine = lax.optimization_barrier((ex_acts.reshape(e_rows, input_cols), *mine))
    both = ("dp", "groups") if share else "dp"
    full = [lax.all_gather(mine[0], both, axis=1, tiled=True)]

    w = weights(eigenvalues)
    acts, ids = [acts], [ex_ids]
    for k in range(1, n):
        last = step_along(acts[-1], n), step_along(ids[-1], n)
        if k == 2:
            *last, w = lax.optimization_barrier((*last, w))
        else:
            last = lax.optimization_barrier(last)
        acts.append(last[0])
        ids.append(last[1])
    all_ids = jnp.concatenate(ids)

    keep = ex_mask.astype(BF).reshape(e_rows, 1, 1)
    e_raw = jnp.transpose(ex_grads.reshape(e_rows, blocks, width) * keep, (1, 0, 2))
    q_raw = jnp.transpose(query_grads.reshape(q_rows, blocks, width), (1, 0, 2))
    xs = ring(e_raw, n)
    if len(mine) > 1:
        xs[-1], *later = lax.optimization_barrier((xs[-1], *mine[1:]))
        full += [lax.all_gather(part, both, axis=1, tiled=True) for part in later]
    zs = [swap(x, "sub") for x in xs]
    q_oth = swap(q_raw, "sub")

    q_in = sum_features(dot(query_acts.reshape(q_rows, input_cols), input_basis), sub, sizes)
    qit = jnp.transpose(q_in.reshape(q_rows // 128, 128, j_rows), (0, 2, 1))
    ei = sum_features(dot(jnp.concatenate(acts, 0), input_basis), sub, sizes)

    total = 0.0
    for i, basis in enumerate(full):
        total = total + chunk_scores(
            n, q_count, seq, i * chunk, idx, ei, qit, w, basis, q_raw, q_oth, xs, zs
        )
    scores = total.sum(2)

    ex_total = all_ids.shape[0]
    onehot = (all_ids[:, None] == jnp.arange(ex_total, dtype=jnp.int32)[None, :]).astype(F32)
    placed = jnp.dot(scores, onehot, precision=lax.Precision.HIGHEST, preferred_element_type=F32)
    if sizes["owner"] == 2:
        pairs = [[(i, i ^ k) for i in range(4)] for k in (1, 2, 3)]
        placed = placed + sum(lax.ppermute(placed, ("owner", "sub"), p) for p in pairs)
    else:
        placed = lax.psum(placed, ("owner", "sub"))

    def columns(device):
        return lax.dynamic_slice_in_dim(placed, lax.rem(device, n) * ex_count, ex_count, 1)

    result = columns(dpi)
    for k in range(1, n):
        pairs = [(i, (i + k) % n) for i in range(n)]
        result = result + lax.ppermute(columns(dpi + k), "dp", pairs)
    return result


def solution(mesh):
    in_specs = (
        P(("groups", "dp"), None, ("owner", "sub")),
        P(("groups", "dp"), None, "owner", "sub"),
        P(("groups", "dp"), None),
        P(("groups", "dp")),
        P("groups", None, ("owner", "sub")),
        P("groups", None, "owner", "sub"),
        P(("owner", "sub"), "dp"),
        P("owner", "dp", "sub"),
        P("dp", "owner", "sub"),
    )
    out_specs = P("groups", "dp")
    body = functools.partial(shards, dict(mesh.shape))
    return jax.shard_map(body, mesh=mesh, in_specs=in_specs, out_specs=out_specs, check_vma=False)
```
